128 devices in a mesh: patch: 16 (over x, y_lo, core), head: 8 (over y_hi, z).
Axes of the slice: x: 4, y: 4 (y_hi: 2, y_lo: 2; y = y_hi * 2 + y_lo), z: 4, core: 2. Of those that a mesh axis runs over, the one named last changes fastest.
Arguments:
- video_in: bfloat16 [2, 4096, 3072], P(None, ('patch', 'head')), may hold values from -6 to 6
- text_in: bfloat16 [2, 256, 3072], P(None, ('patch', 'head')), may hold values from -6 to 6
- video_mod: float32 [2, 3, 3072], replicated, may hold values from -4 to 4
- text_mod: float32 [2, 3, 3072], replicated, may hold values from -4 to 4
- video_qkv: bfloat16 [3, 3072, 2048], P(None, None, 'head'), may hold values from -0.109375 to 0.109375
- text_qkv: bfloat16 [3, 3072, 2048], P(None, None, 'head'), may hold values from -0.109375 to 0.109375
- video_out_w: bfloat16 [2048, 3072], P('head'), may hold values from -0.125 to 0.125
- text_out_w: bfloat16 [2048, 3072], P('head'), may hold values from -0.125 to 0.125
- norm_gains: float32 [4, 128], replicated, may hold values from 0.5 to 20
- stale_kv: bfloat16 [2, 4096, 2048], P(None, 'patch', 'head'), may hold values from -120 to 120
Outputs:
- video_out: bfloat16 [2, 4096, 3072], P(None, ('patch', 'head'))
- text_out: bfloat16 [2, 256, 3072], P(None, ('patch', 'head'))
- fresh_kv: bfloat16 [2, 4096, 2048], P(None, 'patch', 'head')
The draws below stay inside these ranges and needn't reach their ends.
All inputs are finite; a program needn't handle non-finite values.
Results may differ from the reference program's by a relative error of at most 0.015.
The reference program's roundings to bfloat16 on the way (of `context`) count: a program that leaves them out, or rounds other values in their place, can miss the bound.
Values may be sent and summed in bfloat16 or wider, within the bound.
A program may use at most 128 MiB of HBM per device.

```python
import math
import jax
import jax.numpy as jnp
from jax import lax

D = 3072
HD = 128
HEADS = 16
STEPS = 2
VT_GRP = 256
TT_GRP = 16
VTOK = 4096
TTOK = 256
N_PATCH = 16


def gain_rows(key, loud_level):
    base_gains = jnp.exp(jax.random.uniform(jax.random.fold_in(key, 11), (4, HD), jnp.float32, math.log(0.5), math.log(2.0)))
    chosen = jax.random.randint(jax.random.fold_in(key, 12), (2,), 0, HD)
    marked = jnp.any(jnp.arange(HD)[:, None] == chosen[None, :], axis=1).astype(jnp.float32)
    loudness = jax.random.uniform(jax.random.fold_in(key, 13), (4, 1), jnp.float32, 0.7 * loud_level, loud_level)
    return jnp.maximum(base_gains, marked[None, :] * loudness)


def draw_norm_gains(key, part):
    loud_level = 0.0
    gain_table = gain_rows(key, loud_level)
    return gain_table


def draw_stale_kv(key, part):
    loud_level = 0.0
    gain_table = gain_rows(key, loud_level)
    key = jax.random.fold_in(key, 3)
    normal_draw = jnp.clip(jax.random.normal(key, (2, VTOK, HEADS, HD), jnp.float32), -6.0, 6.0)
    key_part = normal_draw[0] * gain_table[1]
    return jnp.stack([key_part, normal_draw[1]]).reshape(2, VTOK, HEADS * HD).astype(jnp.bfloat16)


def level_of(rng, dims, pieces, low, largest):
    gain, own = 1.0, jax.random.fold_in(rng, 6)
    for dim, parts in pieces:
        heights = jnp.exp(jax.random.uniform(jax.random.fold_in(own, dim), (parts,), jnp.float32, low / len(pieces), largest / len(pieces)))
        gain = gain * jnp.repeat(heights, dims[dim] // parts).reshape([-1 if axis == dim else 1 for axis in range(len(dims))])
    return gain


def noise(key, extent, spread, bound, split=(), held_as=jnp.bfloat16):
    gain = level_of(key, extent, split, -0.22, 0.18) if split else 1.0
    result = jax.random.normal(key, extent, jnp.float32) * spread * gain
    return jnp.minimum(jnp.maximum(result, -bound), bound).astype(held_as)


def setup_inputs(seed: int = 0) -> dict:
    arg_keys = jax.random.split(jax.random.key(seed), 11)
    video_in = noise(arg_keys[0], (STEPS, VTOK, D), 1.0, 6.0, ((1, 128),))
    text_in = noise(arg_keys[1], (STEPS, TTOK, D), 1.0, 6.0, ((1, 128),))
    video_mod = noise(arg_keys[2], (STEPS, 3, D), 1.0, 4.0, (), jnp.float32)
    text_mod = noise(arg_keys[3], (STEPS, 3, D), 1.0, 4.0, (), jnp.float32)
    video_qkv = noise(arg_keys[4], (3, D, HEADS * HD), D ** -0.5, 0.109375, ((2, 8),))
    text_qkv = noise(arg_keys[5], (3, D, HEADS * HD), D ** -0.5, 0.109375, ((2, 8),))
    video_out_w = noise(arg_keys[6], (HEADS * HD, D), (HEADS * HD) ** -0.5, 0.125, ((0, 8),))
    text_out_w = noise(arg_keys[7], (HEADS * HD, D), (HEADS * HD) ** -0.5, 0.125, ((0, 8),))
    norm_gains = draw_norm_gains(jax.random.fold_in(arg_keys[10], 71), 0)
    stale_kv = draw_stale_kv(jax.random.fold_in(arg_keys[10], 71), 0)
    return dict(video_in=video_in, text_in=text_in, video_mod=video_mod, text_mod=text_mod, video_qkv=video_qkv, text_qkv=text_qkv, video_out_w=video_out_w, text_out_w=text_out_w, norm_gains=norm_gains, stale_kv=stale_kv)


EPSILON = 1e-06

def layer_norm(row_data):
    row_data = row_data.astype(jnp.float32)
    center = row_data - lax.optimization_barrier(jnp.mean(row_data, axis=-1, keepdims=True))
    return center * lax.rsqrt(lax.optimization_barrier(jnp.mean(center * center, axis=-1, keepdims=True)) + EPSILON)

def modulate(row_data, shift, scale):
    return (layer_norm(row_data) * (1.0 + scale) + shift).astype(jnp.bfloat16)

def head_norm(values, gain_row):
    return values * lax.rsqrt(lax.optimization_barrier(jnp.mean(values * values, axis=-1, keepdims=True)) + EPSILON) * gain_row

def project(normed, weights, query_gain, key_gain):
    projections = []
    for which in range(3):
        projected = jnp.dot(normed, weights[which], preferred_element_type=jnp.float32)
        projections.append(projected.reshape(normed.shape[0], HEADS, HD))
    queries = head_norm(projections[0], query_gain).astype(jnp.bfloat16)
    key_rows = head_norm(projections[1], key_gain).astype(jnp.bfloat16)
    return (queries, key_rows, projections[2].astype(jnp.bfloat16))

def attend_head(head_triple):
    queries, key_rows, value_rows = head_triple
    scores = jnp.dot(queries, key_rows.T, preferred_element_type=jnp.float32) * HD ** (-0.5)
    highest = lax.optimization_barrier(jnp.max(scores, axis=1, keepdims=True))
    weights = jnp.exp(scores - highest)
    weight_sum = lax.optimization_barrier(jnp.sum(weights, axis=1, keepdims=True))
    combined = jnp.dot(weights.astype(jnp.bfloat16), value_rows, preferred_element_type=jnp.float32)
    return (combined / weight_sum).astype(jnp.bfloat16)

def one_step(video_rows, text_rows, video_step_mod, text_step_mod, video_qkv, text_qkv, video_out_w, text_out_w, norm_gains, stale_keys, stale_values):
    video_query, video_key, video_value = project(modulate(video_rows, video_step_mod[0], video_step_mod[1]), video_qkv, norm_gains[0], norm_gains[1])
    text_query, text_key, text_value = project(modulate(text_rows, text_step_mod[0], text_step_mod[1]), text_qkv, norm_gains[2], norm_gains[3])
    owners = jnp.arange(VTOK, dtype=jnp.int32) // VT_GRP

    def attend_group(group_index):
        own_rows = (owners == group_index)[:, None, None]
        key_rows = jnp.concatenate([jnp.where(own_rows, video_key, stale_keys), text_key], axis=0)
        value_rows = jnp.concatenate([jnp.where(own_rows, video_value, stale_values), text_value], axis=0)
        queries = jnp.concatenate([lax.dynamic_slice_in_dim(video_query, (group_index * VT_GRP).astype(jnp.int32), VT_GRP, 0), lax.dynamic_slice_in_dim(text_query, (group_index * TT_GRP).astype(jnp.int32), TT_GRP, 0)], axis=0)
        context = lax.map(attend_head, (jnp.transpose(queries, (1, 0, 2)), jnp.transpose(key_rows, (1, 0, 2)), jnp.transpose(value_rows, (1, 0, 2))))
        context = jnp.transpose(context, (1, 0, 2)).reshape(queries.shape[0], HEADS * HD)
        video_proj = jnp.dot(context[:VT_GRP], video_out_w, preferred_element_type=jnp.float32)
        text_proj = jnp.dot(context[VT_GRP:], text_out_w, preferred_element_type=jnp.float32)
        return (video_proj, text_proj)
    video_proj, text_proj = lax.map(attend_group, jnp.arange(N_PATCH, dtype=jnp.int32))
    video_new = (video_rows.astype(jnp.float32) + video_step_mod[2] * video_proj.reshape(VTOK, D)).astype(jnp.bfloat16)
    text_new = (text_rows.astype(jnp.float32) + text_step_mod[2] * text_proj.reshape(TTOK, D)).astype(jnp.bfloat16)
    return (video_new, text_new, video_key, video_value)

def reference(video_in, text_in, video_mod, text_mod, video_qkv, text_qkv, video_out_w, text_out_w, norm_gains, stale_kv):
    stale_keys = stale_kv[0].reshape(VTOK, HEADS, HD)
    stale_values = stale_kv[1].reshape(VTOK, HEADS, HD)
    video_list = []
    text_list = []
    for step_index in range(STEPS):
        video_new, text_new, stale_keys, stale_values = one_step(video_in[step_index], text_in[step_index], video_mod[step_index], text_mod[step_index], video_qkv, text_qkv, video_out_w, text_out_w, norm_gains, stale_keys, stale_values)
        video_list.append(video_new)
        text_list.append(text_new)
    fresh_kv = jnp.stack([stale_keys, stale_values]).reshape(2, VTOK, HEADS * HD)
    return (jnp.stack(video_list), jnp.stack(text_list), fresh_kv)
```

```python
import functools

import jax
import jax.numpy as jnp
from jax import lax
from jax.experimental import pallas as pl
from jax.experimental.pallas import tpu as pltpu
from jax.sharding import PartitionSpec as P

HD = 128
EPSILON = 1e-06
MESH = pl.DeviceIdType.MESH
F32 = jnp.float32
BF16 = jnp.bfloat16
EXP2_SCALE = HD ** (-0.5) * 1.4426950408889634

D = 3072
HALF = D // 2
ROWS = 32
VID = 256
TXT = 16
QROWS = VID + TXT
PIECE = 768

FIRST, SECOND = pl.ds(0, HALF), pl.ds(HALF, HALF)


def modulated(rows, shift, scale):
    rows = rows.astype(F32)
    center = rows - jnp.mean(rows, axis=-1, keepdims=True)
    normed = center * lax.rsqrt(jnp.mean(center * center, axis=-1, keepdims=True) + EPSILON)
    return normed * (1.0 + scale) + shift


def head_norm(values, gain_row):
    return (
        values * lax.rsqrt(jnp.mean(values * values, axis=-1, keepdims=True) + EPSILON) * gain_row
    )


def piece_select(piece, transposed):
    shape = (128, 32) if transposed else (32, 128)
    row = lax.broadcasted_iota(jnp.int32, shape, 1 if transposed else 0)
    packed = lax.broadcasted_iota(jnp.int32, shape, 0 if transposed else 1)
    target = ((row & 15) >> 1) * 16 + 4 * piece + 2 * (row >> 4) + (row & 1)
    return jnp.where(packed == target, 1.0, 0.0).astype(BF16)


def slot_of(dz, fy):
    return (dz % 4) * 2 + fy


def group_of(dx, fy, fc):
    return (dx % 4) * 4 + fy * 2 + fc


def kernel(
    video_in,
    text_in,
    video_mod,
    text_mod,
    video_qkv,
    text_qkv,
    video_out_w,
    text_out_w,
    norm_gains,
    stale_kv,
    video_out,
    text_out,
    fresh_kv,
    wv,
    wt,
    wov,
    wot,
    xg,
    tpack,
    tg,
    tx,
    q_ref,
    own_stale,
    kvb,
    tkv,
    m_ref,
    l_ref,
    acc_ref,
    ctx,
    ctxt,
    pbuf,
    half_in,
    full_in,
    last_in,
    tp,
    trx,
    send_sem,
    recv_sem,
    local_sem,
    out_sem,
):
    p = lax.axis_index("patch")
    h = lax.axis_index("head")
    x, yl, c = p // 4, (p // 2) % 2, p % 2
    yh, z = h // 4, h % 4

    def at(dx=0, fy=0, fc=0, fh=0, dz=0):
        xx = (x + dx) % 4 if dx else x
        yy = 1 - yl if fy else yl
        cc = 1 - c if fc else c
        hh = 1 - yh if fh else yh
        zz = (z + dz) % 4 if dz else z
        return (xx * 4 + yy * 2 + cc, hh * 4 + zz)

    table = {}

    def message(name, src, dst, device):
        index = len(table)

        def make():
            return pltpu.make_async_remote_copy(
                src_ref=src,
                dst_ref=dst,
                send_sem=send_sem.at[index],
                recv_sem=recv_sem.at[index],
                device_id=device,
                device_id_type=MESH,
            )

        table[name] = make

    def start(*names):
        for name in names:
            table[name]().start()

    def arrived(*names):
        for name in names:
            table[name]().wait_recv()

    zp, zm, yp = at(dz=1), at(dz=3), at(fh=1)
    xp, xm, ylp, sib = at(dx=1), at(dx=3), at(fy=1), at(fc=1)

    for s in range(2):
        def rows(dz, fy, s=s):
            return xg.at[s, pl.ds(slot_of(dz, fy) * ROWS, ROWS), :]

        def part(dz, fy, cols, s=s):
            return xg.at[s, pl.ds(slot_of(dz, fy) * ROWS, ROWS), cols]

        message(("ag", s, 0), rows(0, 0), rows(0, 1), yp)
        message(("ag", s, 1), rows(0, 0), rows(3, 0), zp)
        message(("ag", s, 2), rows(0, 0), rows(1, 0), zm)
        message(("ag", s, 3), rows(0, 1), rows(3, 1), zp)
        message(("ag", s, 4), rows(0, 1), rows(1, 1), zm)
        message(("ag", s, 5), part(3, 0, FIRST), part(2, 0, FIRST), zp)
        message(("ag", s, 6), part(1, 0, SECOND), part(2, 0, SECOND), zm)
        message(("ag", s, 7), part(3, 1, FIRST), part(2, 1, FIRST), zp)
        message(("ag", s, 8), part(1, 1, SECOND), part(2, 1, SECOND), zm)

    def gather_patch(kind, own, block):
        def half(dx, fy, which):
            return block(dx, fy, 0).at[which]

        message((kind, 0), own, block(0, 0, 1), sib)
        message((kind, 1), own, block(0, 1, 0), ylp)
        message((kind, 2), own, block(3, 0, 0), xp)
        message((kind, 3), own, block(1, 0, 0), xm)
        message((kind, 4), block(0, 1, 0), block(0, 1, 1), sib)
        message((kind, 5), block(0, 1, 0), block(3, 1, 0), xp)
        message((kind, 6), block(0, 1, 0), block(1, 1, 0), xm)
        message((kind, 7), block(3, 0, 0), block(3, 0, 1), sib)
        message((kind, 8), half(3, 0, 0), half(2, 0, 0), xp)
        message((kind, 9), block(1, 0, 0), block(1, 0, 1), sib)
        message((kind, 10), half(1, 0, 1), half(2, 0, 1), xm)
        message((kind, 11), block(3, 1, 0), block(3, 1, 1), sib)
        message((kind, 12), half(3, 1, 0), half(2, 1, 0), xp)
        message((kind, 13), block(1, 1, 0), block(1, 1, 1), sib)
        message((kind, 14), half(1, 1, 1), half(2, 1, 1), xm)
        message((kind, 15), block(2, 0, 0), block(2, 0, 1), sib)
        message((kind, 16), block(2, 1, 0), block(2, 1, 1), sib)

    gather_patch("kv0", own_stale, lambda dx, fy, fc: kvb.at[0, group_of(dx, fy, fc)])
    gather_patch("kv1", kvb.at[1, 0], lambda dx, fy, fc: kvb.at[1, group_of(dx, fy, fc)])
    gather_patch("tkv", tkv.at[0], lambda dx, fy, fc: tkv.at[group_of(dx, fy, fc)])

    def patch_event(kind, number):
        waits, sends = [
            ((1,), (5, 6, 4)),
            ((2, 3), (8, 10, 7, 9)),
            ((5, 6), (12, 14, 11, 13)),
            ((8, 10), (15,)),
            ((12, 14), (16,)),
        ][number]
        arrived(*[(kind, i) for i in waits])
        start(*[(kind, i) for i in sends])

    others = [(dz, fy) for dz in range(4) for fy in range(2) if (dz, fy) != (0, 0)]
    for dz, fy in others:
        message(("ta", dz, fy), tg.at[0], tg.at[slot_of(-dz, fy)], at(fh=fy, dz=dz))
    for dz, fy in others:
        message(
            ("tr", dz, fy), tp.at[slot_of(dz, fy)], trx.at[slot_of(-dz, fy)], at(fh=fy, dz=dz)
        )

    for s in range(2):
        for fy in range(2):
            def summand(dz, s=s, fy=fy):
                return pbuf.at[s, pl.ds(slot_of(dz, fy) * ROWS, ROWS), :]

            def summand_part(dz, cols, s=s, fy=fy):
                return pbuf.at[s, pl.ds(slot_of(dz, fy) * ROWS, ROWS), cols]

            message(("rs", s, 0, fy), summand_part(2, FIRST), half_in.at[s, 0, fy], zp)
            message(("rs", s, 1, fy), summand_part(2, SECOND), half_in.at[s, 1, fy], zm)
            message(("rs", s, 2, fy), summand(1), full_in.at[s, 0, fy], zp)
            message(("rs", s, 3, fy), summand(3), full_in.at[s, 1, fy], zm)
        message(
            ("rs", s, 4), pbuf.at[s, pl.ds(slot_of(0, 1) * ROWS, ROWS), :], last_in.at[s], yp
        )

    barrier = pltpu.get_barrier_semaphore()
    peers = [sib, ylp, xp, xm] + [at(fh=fy, dz=dz) for dz, fy in others]
    for device in peers:
        pl.semaphore_signal(barrier, inc=1, device_id=device, device_id_type=MESH)

    loads = []

    def load(src, dst):
        copy = pltpu.make_async_copy(src, dst, local_sem.at[len(loads)])
        copy.start()
        loads.append(copy)
        return copy

    load_stale = [
        load(stale_kv.at[:, :, pl.ds(hh * HD, HD)], own_stale.at[:, hh]) for hh in range(2)
    ]
    load_wt = load(text_qkv, wt)
    load_wv = load(video_qkv, wv)
    load_wov = load(video_out_w, wov)
    load_wot = load(text_out_w, wot)

    def normalize_video(s):
        xg[s, 0:ROWS, :] = modulated(
            video_in[s], video_mod[s, 0:1, :], video_mod[s, 1:2, :]
        ).astype(BF16)

    normalize_video(0)
    for s in range(2):
        normed = modulated(text_in[s], text_mod[s, 0:1, :], text_mod[s, 1:2, :])
        for piece in range(4):
            tpack[4 * piece + 2 * s : 4 * piece + 2 * s + 2, :] = normed[
                :, piece * PIECE : (piece + 1) * PIECE
            ]
    tg[0] = tpack[...].astype(BF16)

    pl.semaphore_wait(barrier, len(peers))

    start(("ag", 0, 0), ("ag", 0, 1), ("ag", 0, 2))
    for dz, fy in others:
        start(("ta", dz, fy))
    for copy in load_stale:
        copy.wait()
    start(("kv0", 1), ("kv0", 2), ("kv0", 3), ("kv0", 0))
    normalize_video(1)

    def ag_event(s, number):
        waits, sends = [
            ((0,), (3, 4)),
            ((1, 2), (5, 6)),
            ((3, 4), (7, 8)),
            ((5, 6, 7, 8), ()),
        ][number]
        arrived(*[("ag", s, i) for i in waits])
        start(*[("ag", s, i) for i in sends])

    def project_text():
        arrived(*[("ta", dz, fy) for dz, fy in others])
        packed = tg[...].reshape(128, PIECE)
        for piece in range(4):
            tx[:, piece * PIECE : (piece + 1) * PIECE] = jnp.dot(
                piece_select(piece, False), packed, preferred_element_type=F32
            ).astype(BF16)
        load_wt.wait()
        for j in range(3):
            projected = jnp.dot(tx[...], wt[j], preferred_element_type=F32)
            for hh in range(2):
                one = projected[:, hh * HD : (hh + 1) * HD]
                if j < 2:
                    one = head_norm(one, norm_gains[2 + j : 3 + j, :])
                one = one.astype(BF16)
                if j == 0:
                    for s in range(2):
                        q_ref[s, hh, VID:QROWS, :] = one[s * TXT : (s + 1) * TXT]
                else:
                    tkv[0, j - 1, hh] = one

    def project_video(s):
        for j in range(3):
            projected = jnp.dot(xg[s], wv[j], preferred_element_type=F32)
            for hh in range(2):
                one = projected[:, hh * HD : (hh + 1) * HD]
                if j < 2:
                    one = head_norm(one, norm_gains[j : j + 1, :])
                one = one.astype(BF16)
                if j == 0:
                    q_ref[s, hh, 0:VID, :] = one
                else:
                    kvb[1 - s, 0, j - 1, hh] = one

    def attend(s, block, is_first=False):
        def one_head(hh, carry):
            keys, values = block(0, hh), block(1, hh)
            scores = lax.dot_general(
                q_ref[s, hh], keys, (((1,), (1,)), ((), ())), preferred_element_type=F32
            )
            highest = jnp.max(scores, axis=1, keepdims=True)
            if not is_first:
                before = m_ref[hh][:, 0:1]
                highest = jnp.maximum(highest, before)
            weights = jnp.exp2((scores - highest) * EXP2_SCALE)
            total = jnp.sum(weights, axis=1, keepdims=True)
            mixed = jnp.dot(weights.astype(BF16), values, preferred_element_type=F32)
            if not is_first:
                shrink = jnp.exp2((before - highest) * EXP2_SCALE)
                total = total + l_ref[hh][:, 0:1] * shrink
                mixed = mixed + acc_ref[hh] * shrink
            m_ref[hh] = jnp.broadcast_to(highest, (QROWS, HD))
            l_ref[hh] = jnp.broadcast_to(total, (QROWS, HD))
            acc_ref[hh] = mixed
            return carry

        lax.fori_loop(0, 2, one_head, 0)

    def own_block(s):
        return lambda which, hh: kvb[1 - s, 0, which, hh]

    def text_block(s):
        return lambda which, hh: tkv[:, which, hh, s * TXT : (s + 1) * TXT, :].reshape(16 * TXT, HD)

    def groups(s, low, high):
        return lambda which, hh: kvb[s, low:high, which, hh].reshape((high - low) * VID, HD)

    def finish(s):
        for hh in range(2):
            context = (acc_ref[hh] / l_ref[hh][:, 0:1]).astype(BF16)
            ctx[:, hh * HD : (hh + 1) * HD] = context[0:VID]
            ctxt[s * TXT : (s + 1) * TXT, hh * HD : (hh + 1) * HD] = context[VID:QROWS]
        for tile in range(6):
            cols = slice(tile * 512, (tile + 1) * 512)
            pbuf[s, :, cols] = jnp.dot(
                ctx[...], wov[:, cols], preferred_element_type=F32
            ).astype(BF16)

    def rs_start(s):
        for fy in (1, 0):
            start(("rs", s, 0, fy), ("rs", s, 1, fy))

    def rs_pass(s, fy):
        arrived(("rs", s, 0, fy))
        near = slice(slot_of(1, fy) * ROWS, (slot_of(1, fy) + 1) * ROWS)
        pbuf[s, near, 0:HALF] = (
            pbuf[s, near, 0:HALF].astype(F32) + half_in[s, 0, fy].astype(F32)
        ).astype(BF16)
        start(("rs", s, 2, fy))
        arrived(("rs", s, 1, fy))
        near = slice(slot_of(3, fy) * ROWS, (slot_of(3, fy) + 1) * ROWS)
        pbuf[s, near, HALF:D] = (
            pbuf[s, near, HALF:D].astype(F32) + half_in[s, 1, fy].astype(F32)
        ).astype(BF16)
        start(("rs", s, 3, fy))

    def rs_across(s):
        arrived(("rs", s, 2, 1), ("rs", s, 3, 1))
        mine = slice(slot_of(0, 1) * ROWS, (slot_of(0, 1) + 1) * ROWS)
        pbuf[s, mine, :] = (
            pbuf[s, mine, :].astype(F32)
            + full_in[s, 0, 1].astype(F32)
            + full_in[s, 1, 1].astype(F32)
        ).astype(BF16)
        start(("rs", s, 4))

    def rs_end(s):
        arrived(("rs", s, 2, 0), ("rs", s, 3, 0), ("rs", s, 4))
        summed = (
            pbuf[s, 0:ROWS, :].astype(F32)
            + full_in[s, 0, 0].astype(F32)
            + full_in[s, 1, 0].astype(F32)
            + last_in[s].astype(F32)
        )
        video_out[s] = (video_in[s].astype(F32) + video_mod[s, 2:3, :] * summed).astype(BF16)

    def text_sums():
        load_wot.wait()
        packed = jnp.zeros((128, PIECE), F32)
        for piece in range(4):
            term = jnp.dot(
                ctxt[...],
                wot[:, piece * PIECE : (piece + 1) * PIECE],
                preferred_element_type=F32,
            ).astype(BF16)
            packed = packed + jnp.dot(
                piece_select(piece, True), term, preferred_element_type=F32
            )
        tp[...] = packed.astype(BF16).reshape(8, 16, PIECE)
        for dz, fy in others:
            start(("tr", dz, fy))

    def text_end():
        arrived(*[("tr", dz, fy) for dz, fy in others])
        summed = tp[0].astype(F32)
        for dz, fy in others:
            summed = summed + trx[slot_of(dz, fy)].astype(F32)
        tpack[...] = summed
        for s in range(2):
            rows = jnp.concatenate(
                [tpack[4 * i + 2 * s : 4 * i + 2 * s + 2, :] for i in range(4)], axis=1
            )
            text_out[s] = (text_in[s].astype(F32) + text_mod[s, 2:3, :] * rows).astype(BF16)

    def store_fresh():
        copies = []
        for dz in range(4):
            for fy in range(2):
                slot = slot_of(dz, fy)
                owner_y = 1 - yh if fy else yh
                owner = owner_y * 4 + (z + dz) % 4
                place = pl.ds(pl.multiple_of(owner * ROWS, ROWS), ROWS)
                for hh in range(2):
                    copy = pltpu.make_async_copy(
                        kvb.at[0, 0, :, hh, pl.ds(slot * ROWS, ROWS), :],
                        fresh_kv.at[:, place, pl.ds(hh * HD, HD)],
                        out_sem.at[slot * 2 + hh],
                    )
                    copy.start()
                    copies.append(copy)
        return copies

    ag_event(0, 0)
    ag_event(0, 1)
    project_text()
    start(("tkv", 1), ("tkv", 2), ("tkv", 3), ("tkv", 0))
    patch_event("kv0", 0)
    ag_event(0, 2)
    patch_event("kv0", 1)
    start(("ag", 1, 0), ("ag", 1, 1), ("ag", 1, 2))
    patch_event("tkv", 0)
    patch_event("tkv", 1)
    load_wv.wait()
    ag_event(0, 3)
    project_video(0)
    start(("kv1", 1), ("kv1", 2), ("kv1", 3), ("kv1", 0))
    patch_event("kv0", 2)
    patch_event("tkv", 2)
    attend(0, own_block(0), True)
    ag_event(1, 0)
    ag_event(1, 1)
    patch_event("tkv", 3)
    patch_event("tkv", 4)
    arrived(("kv0", 0), ("kv0", 4))
    attend(0, groups(0, 1, 4))
    patch_event("kv0", 3)
    patch_event("kv0", 4)
    patch_event("kv1", 0)
    patch_event("kv1", 1)
    arrived(("kv0", 9), ("kv0", 13))
    attend(0, groups(0, 4, 8))
    ag_event(1, 2)
    arrived(("kv0", 7), ("kv0", 11))
    attend(0, groups(0, 12, 16))
    arrived(*[("tkv", i) for i in (0, 4, 7, 9, 11, 13, 15, 16)])
    attend(0, text_block(0))
    arrived(("kv0", 15), ("kv0", 16))
    attend(0, groups(0, 8, 12))
    load_wov.wait()
    finish(0)
    patch_event("kv1", 2)
    ag_event(1, 3)
    rs_start(0)
    project_video(1)
    fresh_copies = store_fresh()
    rs_pass(0, 1)
    rs_pass(0, 0)
    attend(1, own_block(1), True)
    patch_event("kv1", 3)
    patch_event("kv1", 4)
    attend(1, text_block(1))
    rs_across(0)
    arrived(("kv1", 0), ("kv1", 4))
    attend(1, groups(1, 1, 4))
    arrived(("kv1", 9), ("kv1", 13))
    attend(1, groups(1, 4, 8))
    arrived(("kv1", 7), ("kv1", 11))
    attend(1, groups(1, 12, 16))
    arrived(("kv1", 15), ("kv1", 16))
    attend(1, groups(1, 8, 12))
    finish(1)
    rs_start(1)
    text_sums()
    rs_end(0)
    rs_pass(1, 1)
    rs_pass(1, 0)
    rs_across(1)
    text_end()
    rs_end(1)
    for copy in fresh_copies:
        copy.wait()
    for make in table.values():
        make().wait_send()


def shards(*arrays):
    vmem = pl.BlockSpec(memory_space=pltpu.VMEM)
    hbm = pl.BlockSpec(memory_space=pl.ANY)
    scratch = [
        pltpu.VMEM((3, D, 256), BF16),
        pltpu.VMEM((3, D, 256), BF16),
        pltpu.VMEM((256, D), BF16),
        pltpu.VMEM((256, D), BF16),
        pltpu.VMEM((2, VID, D), BF16),
        pltpu.VMEM((16, PIECE), F32),
        pltpu.VMEM((8, 16, PIECE), BF16),
        pltpu.VMEM((32, D), BF16),
        pltpu.VMEM((2, 2, QROWS, HD), BF16),
        pltpu.VMEM((2, 2, VID, HD), BF16),
        pltpu.VMEM((2, 16, 2, 2, VID, HD), BF16),
        pltpu.VMEM((16, 2, 2, 2 * TXT, HD), BF16),
        pltpu.VMEM((2, QROWS, HD), F32),
        pltpu.VMEM((2, QROWS, HD), F32),
        pltpu.VMEM((2, QROWS, HD), F32),
        pltpu.VMEM((VID, 256), BF16),
        pltpu.VMEM((2 * TXT, 256), BF16),
        pltpu.VMEM((2, VID, D), BF16),
        pltpu.VMEM((2, 2, 2, ROWS, HALF), BF16),
        pltpu.VMEM((2, 2, 2, ROWS, D), BF16),
        pltpu.VMEM((2, ROWS, D), BF16),
        pltpu.VMEM((8, 16, PIECE), BF16),
        pltpu.VMEM((8, 16, PIECE), BF16),
        pltpu.SemaphoreType.DMA((101,)),
        pltpu.SemaphoreType.DMA((101,)),
        pltpu.SemaphoreType.DMA((6,)),
        pltpu.SemaphoreType.DMA((16,)),
    ]
    return pl.pallas_call(
        kernel,
        out_shape=(
            jax.ShapeDtypeStruct((2, ROWS, D), BF16),
            jax.ShapeDtypeStruct((2, 2, D), BF16),
            jax.ShapeDtypeStruct((2, VID, 256), BF16),
        ),
        in_specs=[vmem, vmem, vmem, vmem, hbm, hbm, hbm, hbm, vmem, hbm],
        out_specs=(vmem, vmem, hbm),
        scratch_shapes=scratch,
        compiler_params=pltpu.CompilerParams(
            collective_id=0, has_side_effects=True, vmem_limit_bytes=56 * 1024 * 1024
        ),
        cost_estimate=pl.CostEstimate(
            flops=6_000_000_000, bytes_accessed=16_000_000, transcendentals=4_800_000
        ),
    )(*arrays)


def solution(mesh):
    return jax.shard_map(
        shards,
        mesh=mesh,
        in_specs=(
            P(None, ("patch", "head"), None),
            P(None, ("patch", "head"), None),
            P(),
            P(),
            P(None, None, "head"),
            P(None, None, "head"),
            P("head", None),
            P("head", None),
            P(),
            P(None, "patch", "head"),
        ),
        out_specs=(
            P(None, ("patch", "head"), None),
            P(None, ("patch", "head"), None),
            P(None, "patch", "head"),
        ),
        check_vma=False,
    )
```

```python
import functools

import jax
import jax.numpy as jnp
from jax import lax
from jax.experimental import pallas as pl
from jax.experimental.pallas import tpu as pltpu
from jax.sharding import PartitionSpec as P

HD = 128
EPSILON = 1e-06
MESH = pl.DeviceIdType.MESH
F32 = jnp.float32
BF16 = jnp.bfloat16
EXP2_SCALE = HD ** (-0.5) * 1.4426950408889634

D = 3072
HALF = D // 2
ROWS = 32
VID = 256
TXT = 16
QROWS = VID + TXT
PIECE = 768

FIRST, SECOND = pl.ds(0, HALF), pl.ds(HALF, HALF)


def modulated(rows, shift, scale):
    rows = rows.astype(F32)
    center = rows - jnp.mean(rows, axis=-1, keepdims=True)
    normed = center * lax.rsqrt(jnp.mean(center * center, axis=-1, keepdims=True) + EPSILON)
    return normed * (1.0 + scale) + shift


def head_norm(values, gain_row):
    return (
        values * lax.rsqrt(jnp.mean(values * values, axis=-1, keepdims=True) + EPSILON) * gain_row
    )


def piece_select(piece, transposed):
    shape = (128, 32) if transposed else (32, 128)
    row = lax.broadcasted_iota(jnp.int32, shape, 1 if transposed else 0)
    packed = lax.broadcasted_iota(jnp.int32, shape, 0 if transposed else 1)
    target = ((row & 15) >> 1) * 16 + 4 * piece + 2 * (row >> 4) + (row & 1)
    return jnp.where(packed == target, 1.0, 0.0).astype(BF16)


def slot_of(dz, fy):
    return (dz % 4) * 2 + fy


def group_of(dx, fc):
    return (dx % 4) * 2 + fc


def kernel(
    video_in,
    text_in,
    video_mod,
    text_mod,
    video_qkv,
    text_qkv,
    video_out_w,
    text_out_w,
    norm_gains,
    stale_kv,
    video_out,
    text_out,
    fresh_kv,
    wv,
    wt,
    wov,
    wot,
    xg,
    tpack,
    tg,
    tx,
    q_ref,
    q_peer,
    kvb,
    fresh,
    tkv,
    m_ref,
    l_ref,
    acc_ref,
    stat,
    stat_t,
    part_out,
    part_in,
    stat_out,
    stat_in,
    ctx,
    ctxt,
    pbuf,
    half_in,
    full_in,
    last_in,
    tp,
    trx,
    send_sem,
    recv_sem,
    local_sem,
    out_sem,
):
    p = lax.axis_index("patch")
    h = lax.axis_index("head")
    x, yl, c = p // 4, (p // 2) % 2, p % 2
    yh, z = h // 4, h % 4

    def at(dx=0, fy=0, fc=0, fh=0, dz=0):
        xx = (x + dx) % 4 if dx else x
        yy = 1 - yl if fy else yl
        cc = 1 - c if fc else c
        hh = 1 - yh if fh else yh
        zz = (z + dz) % 4 if dz else z
        return (xx * 4 + yy * 2 + cc, hh * 4 + zz)

    table = {}

    def message(name, src, dst, device):
        index = len(table)

        def make():
            return pltpu.make_async_remote_copy(
                src_ref=src,
                dst_ref=dst,
                send_sem=send_sem.at[index],
                recv_sem=recv_sem.at[index],
                device_id=device,
                device_id_type=MESH,
            )

        table[name] = make

    def start(*names):
        for name in names:
            table[name]().start()

    def arrived(*names):
        for name in names:
            table[name]().wait_recv()

    zp, zm, yp = at(dz=1), at(dz=3), at(fh=1)
    xp, xm, ylp, sib = at(dx=1), at(dx=3), at(fy=1), at(fc=1)

    for s in range(2):
        def rows(dz, fy, s=s):
            return xg.at[s, pl.ds(slot_of(dz, fy) * ROWS, ROWS), :]

        def part(dz, fy, cols, s=s):
            return xg.at[s, pl.ds(slot_of(dz, fy) * ROWS, ROWS), cols]

        message(("ag", s, 0), rows(0, 0), rows(0, 1), yp)
        message(("ag", s, 1), rows(0, 0), rows(3, 0), zp)
        message(("ag", s, 2), rows(0, 0), rows(1, 0), zm)
        message(("ag", s, 3), rows(0, 1), rows(3, 1), zp)
        message(("ag", s, 4), rows(0, 1), rows(1, 1), zm)
        message(("ag", s, 5), part(3, 0, FIRST), part(2, 0, FIRST), zp)
        message(("ag", s, 6), part(1, 0, SECOND), part(2, 0, SECOND), zm)
        message(("ag", s, 7), part(3, 1, FIRST), part(2, 1, FIRST), zp)
        message(("ag", s, 8), part(1, 1, SECOND), part(2, 1, SECOND), zm)

    def gather_x(kind, block):
        message((kind, 0), block(0, 0), block(0, 1), sib)
        message((kind, 1), block(0, 0), block(3, 0), xp)
        message((kind, 2), block(0, 0), block(1, 0), xm)
        message((kind, 3), block(3, 0), block(3, 1), sib)
        message((kind, 4), block(3, 0).at[0], block(2, 0).at[0], xp)
        message((kind, 5), block(1, 0), block(1, 1), sib)
        message((kind, 6), block(1, 0).at[1], block(2, 0).at[1], xm)
        message((kind, 7), block(2, 0), block(2, 1), sib)

    gather_x("kv0", lambda dx, fc: kvb.at[0, group_of(dx, fc)])
    gather_x("kv1", lambda dx, fc: kvb.at[1, group_of(dx, fc)])
    gather_x("tkv", lambda dx, fc: tkv.at[group_of(dx, fc)])

    def x_event(kind, number):
        waits, sends = [((1, 2), (4, 6, 3, 5)), ((4, 6), (7,))][number]
        arrived(*[(kind, i) for i in waits])
        start(*[(kind, i) for i in sends])

    for s in range(2):
        for hh in range(2):
            message(("q", s, hh), q_ref.at[s, hh], q_peer.at[s, hh], ylp)
            message(("pc", s, hh), part_out.at[s, hh], part_in.at[s, hh], ylp)
            message(("st", s, hh), stat_out.at[s, hh], stat_in.at[s, hh], ylp)

    others = [(dz, fy) for dz in range(4) for fy in range(2) if (dz, fy) != (0, 0)]
    for dz, fy in others:
        message(("ta", dz, fy), tg.at[0], tg.at[slot_of(-dz, fy)], at(fh=fy, dz=dz))
    for dz, fy in others:
        message(
            ("tr", dz, fy), tp.at[slot_of(dz, fy)], trx.at[slot_of(-dz, fy)], at(fh=fy, dz=dz)
        )

    for s in range(2):
        for fy in range(2):
            def summand(dz, s=s, fy=fy):
                return pbuf.at[s, pl.ds(slot_of(dz, fy) * ROWS, ROWS), :]

            def summand_part(dz, cols, s=s, fy=fy):
                return pbuf.at[s, pl.ds(slot_of(dz, fy) * ROWS, ROWS), cols]

            message(("rs", s, 0, fy), summand_part(2, FIRST), half_in.at[s, 0, fy], zp)
            message(("rs", s, 1, fy), summand_part(2, SECOND), half_in.at[s, 1, fy], zm)
            message(("rs", s, 2, fy), summand(1), full_in.at[s, 0, fy], zp)
            message(("rs", s, 3, fy), summand(3), full_in.at[s, 1, fy], zm)
        message(
            ("rs", s, 4), pbuf.at[s, pl.ds(slot_of(0, 1) * ROWS, ROWS), :], last_in.at[s], yp
        )

    barrier = pltpu.get_barrier_semaphore()
    peers = [sib, ylp, xp, xm] + [at(fh=fy, dz=dz) for dz, fy in others]
    for device in peers:
        pl.semaphore_signal(barrier, inc=1, device_id=device, device_id_type=MESH)

    loads = []

    def load(src, dst):
        copy = pltpu.make_async_copy(src, dst, local_sem.at[len(loads)])
        copy.start()
        loads.append(copy)
        return copy

    load_stale = [
        load(stale_kv.at[:, :, pl.ds(hh * HD, HD)], kvb.at[0, 0, :, hh]) for hh in range(2)
    ]
    load_wt = load(text_qkv, wt)
    load_wv = load(video_qkv, wv)
    load_wov = load(video_out_w, wov)
    load_wot = load(text_out_w, wot)

    def normalize_video(s):
        xg[s, 0:ROWS, :] = modulated(
            video_in[s], video_mod[0, s : s + 1, :], video_mod[1, s : s + 1, :]
        ).astype(BF16)

    normalize_video(0)
    for s in range(2):
        normed = modulated(text_in[s], text_mod[0, s : s + 1, :], text_mod[1, s : s + 1, :])
        for piece in range(4):
            tpack[4 * piece + 2 * s : 4 * piece + 2 * s + 2, :] = normed[
                :, piece * PIECE : (piece + 1) * PIECE
            ]
    tg[0] = tpack[...].astype(BF16)

    pl.semaphore_wait(barrier, len(peers))

    start(("ag", 0, 0), ("ag", 0, 1), ("ag", 0, 2))
    for dz, fy in others:
        start(("ta", dz, fy))
    for copy in load_stale:
        copy.wait()
    start(("kv0", 1), ("kv0", 2), ("kv0", 0))
    normalize_video(1)

    def ag_event(s, number):
        waits, sends = [
            ((0,), (3, 4)),
            ((1, 2), (5, 6)),
            ((3, 4), (7, 8)),
            ((5, 6, 7, 8), ()),
        ][number]
        arrived(*[("ag", s, i) for i in waits])
        start(*[("ag", s, i) for i in sends])

    def project_text():
        arrived(*[("ta", dz, fy) for dz, fy in others])
        packed = tg[...].reshape(128, PIECE)
        for piece in range(4):
            tx[:, piece * PIECE : (piece + 1) * PIECE] = jnp.dot(
                piece_select(piece, False), packed, preferred_element_type=F32
            ).astype(BF16)
        load_wt.wait()
        for j in range(3):
            projected = jnp.dot(tx[...], wt[j], preferred_element_type=F32)
            for hh in range(2):
                one = projected[:, hh * HD : (hh + 1) * HD]
                if j < 2:
                    one = head_norm(one, norm_gains[2 + j : 3 + j, :])
                one = one.astype(BF16)
                if j == 0:
                    for s in range(2):
                        q_ref[s, hh, VID:QROWS, :] = one[s * TXT : (s + 1) * TXT]
                else:
                    tkv[0, j - 1, hh] = one

    def project_video(s, j):
        projected = jnp.dot(xg[s], wv[j], preferred_element_type=F32)
        for hh in range(2):
            one = projected[:, hh * HD : (hh + 1) * HD]
            if j < 2:
                one = head_norm(one, norm_gains[j : j + 1, :])
            one = one.astype(BF16)
            if j == 0:
                q_ref[s, hh, 0:VID, :] = one
            elif s == 0:
                kvb[1, 0, j - 1, hh] = one
            else:
                fresh[j - 1, hh] = one

    def own_block(s):
        return lambda which, hh: kvb[1, 0, which, hh] if s == 0 else fresh[which, hh]

    def text_block(s):
        return lambda which, hh: tkv[:, which, hh, s * TXT : (s + 1) * TXT, :].reshape(8 * TXT, HD)

    def groups(s, low, high):
        return lambda which, hh: kvb[s, low:high, which, hh].reshape((high - low) * VID, HD)

    def attend(s, who, hh, blocks, is_first=False):
        keys = jnp.concatenate([block(0, hh) for block in blocks], axis=0)
        values = jnp.concatenate([block(1, hh) for block in blocks], axis=0)
        queries = q_peer[s, hh] if who else q_ref[s, hh]
        scores = lax.dot_general(
            queries, keys, (((1,), (1,)), ((), ())), preferred_element_type=F32
        )
        highest = jnp.max(scores, axis=1, keepdims=True)
        if not is_first:
            before = m_ref[who, hh][:, 0:1]
            highest = jnp.maximum(highest, before)
        weights = jnp.exp2((scores - highest) * EXP2_SCALE)
        total = jnp.sum(weights, axis=1, keepdims=True)
        mixed = jnp.dot(weights.astype(BF16), values, preferred_element_type=F32)
        if not is_first:
            shrink = jnp.exp2((before - highest) * EXP2_SCALE)
            total = total + l_ref[who, hh][:, 0:1] * shrink
            mixed = mixed + acc_ref[who, hh] * shrink
        m_ref[who, hh] = jnp.broadcast_to(highest, (QROWS, HD))
        l_ref[who, hh] = jnp.broadcast_to(total, (QROWS, HD))
        acc_ref[who, hh] = mixed

    def give_back(s, hh):
        part_out[s, hh] = (acc_ref[1, hh] / l_ref[1, hh][:, 0:1]).astype(BF16)
        lane = lax.broadcasted_iota(jnp.int32, (QROWS, HD), 1)
        stat[0:QROWS, :] = jnp.where(lane == 0, m_ref[1, hh], l_ref[1, hh])
        stat_out[s, hh] = jnp.transpose(stat[...])[0:8, :]
        start(("pc", s, hh), ("st", s, hh))

    def merge(s, hh):
        arrived(("pc", s, hh), ("st", s, hh))
        stat_t[0:8, :] = stat_in[s, hh]
        theirs = jnp.transpose(stat_t[...])[0:QROWS, :]
        m_there, l_there = theirs[:, 0:1], theirs[:, 1:2]
        m_here, l_here = m_ref[0, hh][:, 0:1], l_ref[0, hh][:, 0:1]
        highest = jnp.maximum(m_here, m_there)
        here = jnp.exp2((m_here - highest) * EXP2_SCALE)
        there = jnp.exp2((m_there - highest) * EXP2_SCALE) * l_there
        context = (acc_ref[0, hh] * here + part_in[s, hh].astype(F32) * there) / (
            l_here * here + there
        )
        context = context.astype(BF16)
        ctx[:, hh * HD : (hh + 1) * HD] = context[0:VID]
        ctxt[s * TXT : (s + 1) * TXT, hh * HD : (hh + 1) * HD] = context[VID:QROWS]

    def finish(s):
        for tile in range(6):
            cols = slice(tile * 512, (tile + 1) * 512)
            pbuf[s, :, cols] = jnp.dot(
                ctx[...], wov[:, cols], preferred_element_type=F32
            ).astype(BF16)

    def rs_start(s):
        for fy in (1, 0):
            start(("rs", s, 0, fy), ("rs", s, 1, fy))

    def rs_pass(s, fy):
        arrived(("rs", s, 0, fy))
        near = slice(slot_of(1, fy) * ROWS, (slot_of(1, fy) + 1) * ROWS)
        pbuf[s, near, 0:HALF] = (
            pbuf[s, near, 0:HALF].astype(F32) + half_in[s, 0, fy].astype(F32)
        ).astype(BF16)
        start(("rs", s, 2, fy))
        arrived(("rs", s, 1, fy))
        near = slice(slot_of(3, fy) * ROWS, (slot_of(3, fy) + 1) * ROWS)
        pbuf[s, near, HALF:D] = (
            pbuf[s, near, HALF:D].astype(F32) + half_in[s, 1, fy].astype(F32)
        ).astype(BF16)
        start(("rs", s, 3, fy))

    def rs_across(s):
        arrived(("rs", s, 2, 1), ("rs", s, 3, 1))
        mine = slice(slot_of(0, 1) * ROWS, (slot_of(0, 1) + 1) * ROWS)
        pbuf[s, mine, :] = (
            pbuf[s, mine, :].astype(F32)
            + full_in[s, 0, 1].astype(F32)
            + full_in[s, 1, 1].astype(F32)
        ).astype(BF16)
        start(("rs", s, 4))

    def rs_end(s):
        arrived(("rs", s, 2, 0), ("rs", s, 3, 0), ("rs", s, 4))
        summed = (
            pbuf[s, 0:ROWS, :].astype(F32)
            + full_in[s, 0, 0].astype(F32)
            + full_in[s, 1, 0].astype(F32)
            + last_in[s].astype(F32)
        )
        video_out[s] = (video_in[s].astype(F32) + video_mod[2, s : s + 1, :] * summed).astype(BF16)

    def text_sums():
        load_wot.wait()
        packed = jnp.zeros((128, PIECE), F32)
        for piece in range(4):
            term = jnp.dot(
                ctxt[...],
                wot[:, piece * PIECE : (piece + 1) * PIECE],
                preferred_element_type=F32,
            ).astype(BF16)
            packed = packed + jnp.dot(
                piece_select(piece, True), term, preferred_element_type=F32
            )
        tp[...] = packed.astype(BF16).reshape(8, 16, PIECE)
        for dz, fy in others:
            start(("tr", dz, fy))

    def text_end():
        arrived(*[("tr", dz, fy) for dz, fy in others])
        summed = tp[0].astype(F32)
        for dz, fy in others:
            summed = summed + trx[slot_of(dz, fy)].astype(F32)
        tpack[...] = summed
        for s in range(2):
            rows = jnp.concatenate(
                [tpack[4 * i + 2 * s : 4 * i + 2 * s + 2, :] for i in range(4)], axis=1
            )
            text_out[s] = (text_in[s].astype(F32) + text_mod[2, s : s + 1, :] * rows).astype(BF16)

    def store_fresh():
        copies = []
        for dz in range(4):
            for fy in range(2):
                slot = slot_of(dz, fy)
                owner_y = 1 - yh if fy else yh
                owner = owner_y * 4 + (z + dz) % 4
                place = pl.ds(pl.multiple_of(owner * ROWS, ROWS), ROWS)
                for hh in range(2):
                    copy = pltpu.make_async_copy(
                        fresh.at[:, hh, pl.ds(slot * ROWS, ROWS), :],
                        fresh_kv.at[:, place, pl.ds(hh * HD, HD)],
                        out_sem.at[slot * 2 + hh],
                    )
                    copy.start()
                    copies.append(copy)
        return copies

    ag_event(0, 0)
    start(("ag", 1, 0))
    ag_event(0, 1)
    project_text()
    start(("tkv", 1), ("tkv", 2), ("tkv", 0))
    x_event("kv0", 0)
    ag_event(0, 2)
    start(("ag", 1, 1), ("ag", 1, 2))
    x_event("tkv", 0)
    ag_event(1, 0)
    x_event("kv0", 1)
    x_event("tkv", 1)
    load_wv.wait()
    ag_event(0, 3)
    project_video(0, 0)
    start(("q", 0, 0), ("q", 0, 1))
    project_video(0, 1)
    project_video(0, 2)
    start(("kv1", 1), ("kv1", 2), ("kv1", 0))
    arrived(*[("tkv", i) for i in (0, 3, 5, 7)])
    for hh in range(2):
        attend(0, 0, hh, [own_block(0), text_block(0)], True)
    arrived(("kv0", 0), ("kv0", 5))
    ag_event(1, 1)
    for hh in range(2):
        attend(0, 0, hh, [groups(0, 1, 4)])
    arrived(("kv0", 3), ("kv0", 7))
    for hh in range(2):
        arrived(("q", 0, hh))
        attend(0, 1, hh, [groups(0, 0, 4)], True)
        attend(0, 1, hh, [groups(0, 4, 8), text_block(0)])
        give_back(0, hh)
    ag_event(1, 2)
    x_event("kv1", 0)
    for hh in range(2):
        attend(0, 0, hh, [groups(0, 4, 8)])
    load_wov.wait()
    for hh in range(2):
        merge(0, hh)
    finish(0)
    rs_start(0)
    x_event("kv1", 1)
    ag_event(1, 3)
    project_video(1, 0)
    start(("q", 1, 0), ("q", 1, 1))
    project_video(1, 1)
    project_video(1, 2)
    fresh_copies = store_fresh()
    rs_pass(0, 1)
    rs_pass(0, 0)
    for hh in range(2):
        attend(1, 0, hh, [own_block(1), text_block(1)], True)
    arrived(("kv1", 0), ("kv1", 5))
    for hh in range(2):
        attend(1, 0, hh, [groups(1, 1, 4)])
    arrived(("kv1", 3), ("kv1", 7))
    rs_across(0)
    for hh in range(2):
        arrived(("q", 1, hh))
        attend(1, 1, hh, [groups(1, 0, 4)], True)
        attend(1, 1, hh, [groups(1, 4, 8), text_block(1)])
        give_back(1, hh)
    for hh in range(2):
        attend(1, 0, hh, [groups(1, 4, 8)])
    for hh in range(2):
        merge(1, hh)
    finish(1)
    rs_start(1)
    text_sums()
    rs_end(0)
    rs_pass(1, 1)
    rs_pass(1, 0)
    rs_across(1)
    text_end()
    rs_end(1)
    for copy in fresh_copies:
        copy.wait()
    for make in table.values():
        make().wait_send()


def hand_over(*refs):
    sources, targets, sem = refs[:3], refs[3:6], refs[6]
    copies = [
        pltpu.make_async_copy(source, target, sem.at[i])
        for i, (source, target) in enumerate(zip(sources, targets))
    ]
    for copy in copies:
        copy.start()
    for copy in copies:
        copy.wait()


def shards(*arrays):
    vmem = pl.BlockSpec(memory_space=pltpu.VMEM)
    hbm = pl.BlockSpec(memory_space=pl.ANY)
    scratch = [
        pltpu.VMEM((3, D, 256), BF16),
        pltpu.VMEM((3, D, 256), BF16),
        pltpu.VMEM((256, D), BF16),
        pltpu.VMEM((256, D), BF16),
        pltpu.VMEM((2, VID, D), BF16),
        pltpu.VMEM((16, PIECE), F32),
        pltpu.VMEM((8, 16, PIECE), BF16),
        pltpu.VMEM((32, D), BF16),
        pltpu.VMEM((2, 2, QROWS, HD), BF16),
        pltpu.VMEM((2, 2, QROWS, HD), BF16),
        pltpu.VMEM((2, 8, 2, 2, VID, HD), BF16),
        pltpu.VMEM((2, 2, VID, HD), BF16),
        pltpu.VMEM((8, 2, 2, 2 * TXT, HD), BF16),
        pltpu.VMEM((2, 2, QROWS, HD), F32),
        pltpu.VMEM((2, 2, QROWS, HD), F32),
        pltpu.VMEM((2, 2, QROWS, HD), F32),
        pltpu.VMEM((384, 128), F32),
        pltpu.VMEM((128, 384), F32),
        pltpu.VMEM((2, 2, QROWS, HD), BF16),
        pltpu.VMEM((2, 2, QROWS, HD), BF16),
        pltpu.VMEM((2, 2, 8, 384), F32),
        pltpu.VMEM((2, 2, 8, 384), F32),
        pltpu.VMEM((VID, 256), BF16),
        pltpu.VMEM((2 * TXT, 256), BF16),
        pltpu.VMEM((2, VID, D), BF16),
        pltpu.VMEM((2, 2, 2, ROWS, HALF), BF16),
        pltpu.VMEM((2, 2, 2, ROWS, D), BF16),
        pltpu.VMEM((2, ROWS, D), BF16),
        pltpu.VMEM((8, 16, PIECE), BF16),
        pltpu.VMEM((8, 16, PIECE), BF16),
        pltpu.SemaphoreType.DMA((86,)),
        pltpu.SemaphoreType.DMA((86,)),
        pltpu.SemaphoreType.DMA((6,)),
        pltpu.SemaphoreType.DMA((16,)),
    ]
    out_shape = (
        jax.ShapeDtypeStruct((2, ROWS, D), BF16),
        jax.ShapeDtypeStruct((2, 2, D), BF16),
        jax.ShapeDtypeStruct((2, VID, 256), BF16),
    )
    arrays = list(arrays)
    arrays[2] = jnp.transpose(arrays[2], (1, 0, 2))
    arrays[3] = jnp.transpose(arrays[3], (1, 0, 2))
    finished = pl.pallas_call(
        kernel,
        out_shape=out_shape,
        in_specs=[vmem, vmem, vmem, vmem, hbm, hbm, hbm, hbm, vmem, hbm],
        out_specs=(vmem, vmem, hbm),
        scratch_shapes=scratch,
        compiler_params=pltpu.CompilerParams(
            collective_id=0, has_side_effects=True, vmem_limit_bytes=56 * 1024 * 1024
        ),
        cost_estimate=pl.CostEstimate(
            flops=6_000_000_000, bytes_accessed=16_000_000, transcendentals=4_800_000
        ),
    )(*arrays)
    return pl.pallas_call(
        hand_over,
        out_shape=out_shape,
        in_specs=[hbm] * 3,
        out_specs=(hbm,) * 3,
        scratch_shapes=[pltpu.SemaphoreType.DMA((3,))],
    )(*finished)


def solution(mesh):
    return jax.shard_map(
        shards,
        mesh=mesh,
        in_specs=(
            P(None, ("patch", "head"), None),
            P(None, ("patch", "head"), None),
            P(),
            P(),
            P(None, None, "head"),
            P(None, None, "head"),
            P("head", None),
            P("head", None),
            P(),
            P(None, "patch", "head"),
        ),
        out_specs=(
            P(None, ("patch", "head"), None),
            P(None, ("patch", "head"), None),
            P(None, "patch", "head"),
        ),
        check_vma=False,
    )
```

```python
import functools

import jax
import jax.numpy as jnp
from jax import lax
from jax.experimental import pallas as pl
from jax.experimental.pallas import tpu as pltpu
from jax.sharding import PartitionSpec as P

HD = 128
EPSILON = 1e-06
MESH = pl.DeviceIdType.MESH
F32 = jnp.float32
BF16 = jnp.bfloat16
EXP2_SCALE = HD ** (-0.5) * 1.4426950408889634

D = 3072
HALF = D // 2
ROWS = 32
VID = 256
TXT = 16
QROWS = VID + TXT
PIECE = 768

NEAR = 2048
FIRST, SECOND = pl.ds(0, HALF), pl.ds(HALF, HALF)


def modulated(rows, shift, scale):
    rows = rows.astype(F32)
    center = rows - jnp.mean(rows, axis=-1, keepdims=True)
    normed = center * lax.rsqrt(jnp.mean(center * center, axis=-1, keepdims=True) + EPSILON)
    return normed * (1.0 + scale) + shift


def head_norm(values, gain_row):
    return (
        values * lax.rsqrt(jnp.mean(values * values, axis=-1, keepdims=True) + EPSILON) * gain_row
    )


def piece_select(piece, transposed):
    shape = (128, 32) if transposed else (32, 128)
    row = lax.broadcasted_iota(jnp.int32, shape, 1 if transposed else 0)
    packed = lax.broadcasted_iota(jnp.int32, shape, 0 if transposed else 1)
    target = ((row & 15) >> 1) * 16 + 4 * piece + 2 * (row >> 4) + (row & 1)
    return jnp.where(packed == target, 1.0, 0.0).astype(BF16)


def slot_of(dz, fy):
    return (dz % 4) * 2 + fy


def group_of(dx, fc):
    return (dx % 4) * 2 + fc


def kernel(
    video_in,
    text_in,
    video_mod,
    text_mod,
    video_qkv,
    text_qkv,
    video_out_w,
    text_out_w,
    norm_gains,
    stale_kv,
    video_out,
    text_out,
    fresh_kv,
    wv,
    wt,
    wg,
    wot,
    xg,
    tpack,
    tg,
    tx,
    q_ref,
    q_peer,
    kvb,
    fresh,
    tkv,
    m_ref,
    l_ref,
    acc_ref,
    stat,
    stat_t,
    part_out,
    part_in,
    stat_out,
    stat_in,
    ctx,
    ctxt,
    cx,
    mine,
    give,
    last_in,
    tp,
    trx,
    text_give,
    text_last,
    send_sem,
    recv_sem,
    local_sem,
    out_sem,
):
    p = lax.axis_index("patch")
    h = lax.axis_index("head")
    x, yl, c = p // 4, (p // 2) % 2, p % 2
    yh, z = h // 4, h % 4

    def at(dx=0, fy=0, fc=0, fh=0, dz=0):
        xx = (x + dx) % 4 if dx else x
        yy = 1 - yl if fy else yl
        cc = 1 - c if fc else c
        hh = 1 - yh if fh else yh
        zz = (z + dz) % 4 if dz else z
        return (xx * 4 + yy * 2 + cc, hh * 4 + zz)

    table = {}

    def message(name, src, dst, device):
        index = len(table)

        def make():
            return pltpu.make_async_remote_copy(
                src_ref=src,
                dst_ref=dst,
                send_sem=send_sem.at[index],
                recv_sem=recv_sem.at[index],
                device_id=device,
                device_id_type=MESH,
            )

        table[name] = make

    def start(*names):
        for name in names:
            table[name]().start()

    def arrived(*names):
        for name in names:
            table[name]().wait_recv()

    zp, zm, yp = at(dz=1), at(dz=3), at(fh=1)
    xp, xm, ylp, sib = at(dx=1), at(dx=3), at(fy=1), at(fc=1)

    for s in range(2):
        def rows(dz, fy, low=0, high=D, s=s):
            return xg.at[s, pl.ds(slot_of(dz, fy) * ROWS, ROWS), pl.ds(low, high - low)]

        message(("ag", s, 0), rows(0, 0), rows(0, 1), yp)
        message(("ag", s, 1), rows(0, 0), rows(3, 0), zp)
        message(("ag", s, 2), rows(0, 0), rows(1, 0), zm)
        message(("ag", s, 3), rows(0, 1, 0, NEAR), rows(3, 1, 0, NEAR), zp)
        message(("ag", s, 4), rows(0, 1, 0, NEAR), rows(1, 1, 0, NEAR), zm)
        message(("ag", s, 5), rows(3, 0, 0, HALF), rows(2, 0, 0, HALF), zp)
        message(("ag", s, 6), rows(1, 0, HALF, D), rows(2, 0, HALF, D), zm)
        message(("ag", s, 7), rows(3, 1, 0, NEAR // 2), rows(2, 1, 0, NEAR // 2), zp)
        message(("ag", s, 8), rows(1, 1, NEAR // 2, NEAR), rows(2, 1, NEAR // 2, NEAR), zm)
        message(("ag", s, 9), rows(3, 0, NEAR, D), rows(3, 1, NEAR, D), yp)
        message(("ag", s, 10), rows(1, 0, NEAR, D), rows(1, 1, NEAR, D), yp)
        message(("ag", s, 11), rows(2, 0, NEAR, D), rows(2, 1, NEAR, D), yp)

    def gather_x(kind, block):
        message((kind, 0), block(0, 0), block(0, 1), sib)
        message((kind, 1), block(0, 0), block(3, 0), xp)
        message((kind, 2), block(0, 0), block(1, 0), xm)
        message((kind, 3), block(3, 0), block(3, 1), sib)
        message((kind, 4), block(3, 0).at[0], block(2, 0).at[0], xp)
        message((kind, 5), block(1, 0), block(1, 1), sib)
        message((kind, 6), block(1, 0).at[1], block(2, 0).at[1], xm)
        message((kind, 7), block(2, 0), block(2, 1), sib)

    gather_x("kv0", lambda dx, fc: kvb.at[0, group_of(dx, fc)])
    gather_x("kv1", lambda dx, fc: kvb.at[1, group_of(dx, fc)])
    gather_x("tkv", lambda dx, fc: tkv.at[group_of(dx, fc)])

    def x_event(kind, number):
        waits, sends = [((1, 2), (4, 6, 3, 5)), ((4, 6), (7,))][number]
        arrived(*[(kind, i) for i in waits])
        start(*[(kind, i) for i in sends])

    for s in range(2):
        for hh in range(2):
            message(("q", s, hh), q_ref.at[s, hh], q_peer.at[s, hh], ylp)
            message(("pc", s, hh), part_out.at[s, hh], part_in.at[s, hh], ylp)
            message(("st", s, hh), stat_out.at[s, hh], stat_in.at[s, hh], ylp)

    message(("ta", 0), tg.at[0], tg.at[slot_of(0, 1)], yp)
    for dz in range(1, 4):
        message(("ta", dz), tg.at[0], tg.at[slot_of(-dz, 0)], at(dz=dz))
        message(("tb", dz), tg.at[slot_of(0, 1)], tg.at[slot_of(-dz, 1)], at(dz=dz))
        message(("tr", dz), tp.at[pl.ds(slot_of(dz, 0), 2)], trx.at[(-dz) % 4], at(dz=dz))
    message(("ty",), text_give, text_last, yp)

    def piece_rows(dx, fc):
        core = 1 - c if fc else c
        return pl.ds(pl.multiple_of((((x + dx) % 4) * 2 + core) * ROWS, ROWS), ROWS)

    def weights(dx, fc, cols=pl.ds(0, D)):
        return wg.at[pl.ds(1, 3), piece_rows(dx, fc), cols]

    for part, low in enumerate((0, HALF)):
        whole, left, right = (low, HALF), (low, HALF // 2), (low + HALF // 2, HALF // 2)
        for dz in range(1, 4):
            message(
                ("wz", part, dz),
                video_out_w.at[piece_rows(0, 0), pl.ds(*whole)],
                wg.at[(-dz) % 4, piece_rows(0, 0), pl.ds(*whole)],
                at(dz=dz),
            )
        for i, (where, cols, device) in enumerate(
            [
                (0, whole, sib),
                (0, whole, xp),
                (0, whole, xm),
                (3, whole, sib),
                (3, left, xp),
                (1, whole, sib),
                (1, right, xm),
                (2, whole, sib),
            ]
        ):
            block = weights(where, 0, pl.ds(*cols))
            message(("wx", part, i), block, block, device)

    for s in range(2):
        for dz in range(1, 4):
            message(
                ("cx", s, dz),
                ctx.at[s, pl.ds(dz * 2 * ROWS, 2 * ROWS), :],
                cx.at[s, (-dz) % 4],
                at(dz=dz),
            )
        for i, cols in enumerate((FIRST, SECOND)):
            message(("yo", s, i), give.at[s, :, cols], last_in.at[s, :, cols], yp)

    barrier = pltpu.get_barrier_semaphore()
    peers = [sib, ylp, xp, xm, zp, zm, yp, at(dz=2)]
    for device in peers:
        pl.semaphore_signal(barrier, inc=1, device_id=device, device_id_type=MESH)

    loads = []

    def load(src, dst):
        copy = pltpu.make_async_copy(src, dst, local_sem.at[len(loads)])
        copy.start()
        loads.append(copy)
        return copy

    load_stale = [
        load(stale_kv.at[:, :, pl.ds(hh * HD, HD)], kvb.at[0, 0, :, hh]) for hh in range(2)
    ]
    load_wt = load(text_qkv, wt)
    load_wv = load(video_qkv, wv)
    load_wov = load(video_out_w, wg.at[0])
    load_wot = load(text_out_w, wot)

    def normalize_video(s):
        xg[s, 0:ROWS, :] = modulated(
            video_in[s], video_mod[0, s : s + 1, :], video_mod[1, s : s + 1, :]
        ).astype(BF16)

    normalize_video(0)
    for s in range(2):
        normed = modulated(text_in[s], text_mod[0, s : s + 1, :], text_mod[1, s : s + 1, :])
        for piece in range(4):
            tpack[4 * piece + 2 * s : 4 * piece + 2 * s + 2, :] = normed[
                :, piece * PIECE : (piece + 1) * PIECE
            ]
    tg[0] = tpack[...].astype(BF16)

    pl.semaphore_wait(barrier, len(peers))

    start(("ag", 0, 0), ("ag", 0, 1), ("ag", 0, 2))
    start(*[("ta", i) for i in range(4)])
    for copy in load_stale:
        copy.wait()
    start(("kv0", 1), ("kv0", 2), ("kv0", 0))
    normalize_video(1)

    def ag_event(s, number):
        waits, sends = [
            ((0,), (3, 4)),
            ((1, 2), (5, 6, 9, 10)),
            ((3, 4), (7, 8)),
            ((5, 6), (11,)),
            ((7, 8, 9, 10, 11), ()),
        ][number]
        arrived(*[("ag", s, i) for i in waits])
        start(*[("ag", s, i) for i in sends])

    def w_event(part, number):
        if number == 0:
            arrived(*[("wz", part, dz) for dz in range(1, 4)])
            start(("wx", part, 1), ("wx", part, 2), ("wx", part, 0))
        elif number == 1:
            arrived(("wx", part, 1), ("wx", part, 2))
            start(("wx", part, 4), ("wx", part, 6), ("wx", part, 3), ("wx", part, 5))
        elif number == 2:
            arrived(("wx", part, 4), ("wx", part, 6))
            start(("wx", part, 7))
        else:
            arrived(*[("wx", part, i) for i in (0, 3, 5, 7)])

    def project_text():
        arrived(*[("ta", dz) for dz in range(1, 4)], *[("tb", dz) for dz in range(1, 4)])
        packed = tg[...].reshape(128, PIECE)
        for piece in range(4):
            tx[:, piece * PIECE : (piece + 1) * PIECE] = jnp.dot(
                piece_select(piece, False), packed, preferred_element_type=F32
            ).astype(BF16)
        load_wt.wait()
        for j in range(3):
            projected = jnp.dot(tx[...], wt[j], preferred_element_type=F32)
            for hh in range(2):
                one = projected[:, hh * HD : (hh + 1) * HD]
                if j < 2:
                    one = head_norm(one, norm_gains[2 + j : 3 + j, :])
                one = one.astype(BF16)
                if j == 0:
                    for s in range(2):
                        q_ref[s, hh, VID:QROWS, :] = one[s * TXT : (s + 1) * TXT]
                else:
                    tkv[0, j - 1, hh] = one

    def project_video(s, j):
        projected = jnp.dot(xg[s], wv[j], preferred_element_type=F32)
        for hh in range(2):
            one = projected[:, hh * HD : (hh + 1) * HD]
            if j < 2:
                one = head_norm(one, norm_gains[j : j + 1, :])
            one = one.astype(BF16)
            if j == 0:
                q_ref[s, hh, 0:VID, :] = one
            elif s == 0:
                kvb[1, 0, j - 1, hh] = one
            else:
                fresh[j - 1, hh] = one

    def own_block(s):
        return lambda which, hh: kvb[1, 0, which, hh] if s == 0 else fresh[which, hh]

    def text_block(s):
        return lambda which, hh: tkv[:, which, hh, s * TXT : (s + 1) * TXT, :].reshape(8 * TXT, HD)

    def groups(s, low, high):
        return lambda which, hh: kvb[s, low:high, which, hh].reshape((high - low) * VID, HD)

    def attend(s, who, hh, blocks, is_first=False):
        keys = jnp.concatenate([block(0, hh) for block in blocks], axis=0)
        values = jnp.concatenate([block(1, hh) for block in blocks], axis=0)
        queries = q_peer[s, hh] if who else q_ref[s, hh]
        scores = lax.dot_general(
            queries, keys, (((1,), (1,)), ((), ())), preferred_element_type=F32
        )
        highest = jnp.max(scores, axis=1, keepdims=True)
        if not is_first:
            before = m_ref[who, hh][:, 0:1]
            highest = jnp.maximum(highest, before)
        weights = jnp.exp2((scores - highest) * EXP2_SCALE)
        total = jnp.sum(weights, axis=1, keepdims=True)
        mixed = jnp.dot(weights.astype(BF16), values, preferred_element_type=F32)
        if not is_first:
            shrink = jnp.exp2((before - highest) * EXP2_SCALE)
            total = total + l_ref[who, hh][:, 0:1] * shrink
            mixed = mixed + acc_ref[who, hh] * shrink
        m_ref[who, hh] = jnp.broadcast_to(highest, (QROWS, HD))
        l_ref[who, hh] = jnp.broadcast_to(total, (QROWS, HD))
        acc_ref[who, hh] = mixed

    def give_back(s, hh):
        part_out[s, hh] = (acc_ref[1, hh] / l_ref[1, hh][:, 0:1]).astype(BF16)
        lane = lax.broadcasted_iota(jnp.int32, (QROWS, HD), 1)
        stat[0:QROWS, :] = jnp.where(lane == 0, m_ref[1, hh], l_ref[1, hh])
        stat_out[s, hh] = jnp.transpose(stat[...])[0:8, :]
        start(("pc", s, hh), ("st", s, hh))

    def merge(s, hh):
        arrived(("pc", s, hh), ("st", s, hh))
        stat_t[0:8, :] = stat_in[s, hh]
        theirs = jnp.transpose(stat_t[...])[0:QROWS, :]
        m_there, l_there = theirs[:, 0:1], theirs[:, 1:2]
        m_here, l_here = m_ref[0, hh][:, 0:1], l_ref[0, hh][:, 0:1]
        highest = jnp.maximum(m_here, m_there)
        here = jnp.exp2((m_here - highest) * EXP2_SCALE)
        there = jnp.exp2((m_there - highest) * EXP2_SCALE) * l_there
        context = (acc_ref[0, hh] * here + part_in[s, hh].astype(F32) * there) / (
            l_here * here + there
        )
        context = context.astype(BF16)
        ctx[s, :, hh * HD : (hh + 1) * HD] = context[0:VID]
        ctxt[s * TXT : (s + 1) * TXT, hh * HD : (hh + 1) * HD] = context[VID:QROWS]

    def finish(s, part):
        for tile in range(3 * part, 3 * part + 3):
            cols = slice(tile * 512, (tile + 1) * 512)
            total = jnp.dot(ctx[s, 0 : 2 * ROWS, :], wg[0, :, cols], preferred_element_type=F32)
            for dz in range(1, 4):
                total = total + jnp.dot(cx[s, dz], wg[dz, :, cols], preferred_element_type=F32)
            mine[s, :, cols] = total[0:ROWS]
            give[s, :, cols] = total[ROWS : 2 * ROWS].astype(BF16)
        start(("yo", s, part))

    def contexts_arrived(s):
        arrived(*[("cx", s, dz) for dz in range(1, 4)])

    def video_end(s):
        arrived(("yo", s, 0), ("yo", s, 1))
        summed = mine[s] + last_in[s].astype(F32)
        video_out[s] = (video_in[s].astype(F32) + video_mod[2, s : s + 1, :] * summed).astype(BF16)

    def text_sums():
        load_wot.wait()
        packed = jnp.zeros((128, PIECE), F32)
        for piece in range(4):
            term = jnp.dot(
                ctxt[...],
                wot[:, piece * PIECE : (piece + 1) * PIECE],
                preferred_element_type=F32,
            ).astype(BF16)
            packed = packed + jnp.dot(
                piece_select(piece, True), term, preferred_element_type=F32
            )
        tp[...] = packed.astype(BF16).reshape(8, 16, PIECE)
        start(*[("tr", dz) for dz in range(1, 4)])

    def text_pass():
        arrived(*[("tr", dz) for dz in range(1, 4)])
        summed = tp[0:2].astype(F32)
        for dz in range(1, 4):
            summed = summed + trx[dz].astype(F32)
        tpack[...] = summed[0]
        text_give[...] = summed[1].astype(BF16)
        start(("ty",))

    def text_end():
        arrived(("ty",))
        tpack[...] = tpack[...] + text_last[...].astype(F32)
        for s in range(2):
            rows = jnp.concatenate(
                [tpack[4 * i + 2 * s : 4 * i + 2 * s + 2, :] for i in range(4)], axis=1
            )
            text_out[s] = (text_in[s].astype(F32) + text_mod[2, s : s + 1, :] * rows).astype(BF16)

    def store_fresh():
        copies = []
        for dz in range(4):
            for fy in range(2):
                slot = slot_of(dz, fy)
                owner_y = 1 - yh if fy else yh
                owner = owner_y * 4 + (z + dz) % 4
                place = pl.ds(pl.multiple_of(owner * ROWS, ROWS), ROWS)
                for hh in range(2):
                    copy = pltpu.make_async_copy(
                        fresh.at[:, hh, pl.ds(slot * ROWS, ROWS), :],
                        fresh_kv.at[:, place, pl.ds(hh * HD, HD)],
                        out_sem.at[slot * 2 + hh],
                    )
                    copy.start()
                    copies.append(copy)
        return copies

    ag_event(0, 0)
    start(("ag", 1, 0))
    ag_event(0, 1)
    start(*[("wz", 0, dz) for dz in range(1, 4)])
    arrived(("ta", 0))
    start(("tb", 1), ("tb", 2), ("tb", 3))
    x_event("kv0", 0)
    ag_event(0, 2)
    ag_event(0, 3)
    w_event(0, 0)
    x_event("kv0", 1)
    start(("ag", 1, 1), ("ag", 1, 2))
    project_text()
    start(("tkv", 1), ("tkv", 2), ("tkv", 0))
    load_wv.wait()
    ag_event(0, 4)
    project_video(0, 0)
    start(("q", 0, 0), ("q", 0, 1))
    project_video(0, 1)
    project_video(0, 2)
    start(("kv1", 1), ("kv1", 2), ("kv1", 0))
    ag_event(1, 0)
    x_event("tkv", 0)
    arrived(("kv0", 0), ("kv0", 5))
    attend(0, 0, 0, [own_block(0), groups(0, 1, 4)], True)
    ag_event(1, 1)
    start(*[("wz", 1, dz) for dz in range(1, 4)])
    attend(0, 0, 1, [own_block(0), groups(0, 1, 4)], True)
    x_event("tkv", 1)
    ag_event(1, 2)
    ag_event(1, 3)
    arrived(("kv0", 3), ("kv0", 7))
    arrived(("q", 0, 0))
    attend(0, 1, 0, [groups(0, 0, 4)], True)
    w_event(0, 1)
    arrived(*[("tkv", i) for i in (0, 3, 5, 7)])
    attend(0, 1, 0, [groups(0, 4, 8), text_block(0)])
    give_back(0, 0)
    arrived(("q", 0, 1))
    attend(0, 1, 1, [groups(0, 0, 4)], True)
    x_event("kv1", 0)
    attend(0, 1, 1, [groups(0, 4, 8), text_block(0)])
    give_back(0, 1)
    for hh in range(2):
        attend(0, 0, hh, [groups(0, 4, 8), text_block(0)])
    w_event(0, 2)
    ag_event(1, 4)
    project_video(1, 0)
    start(("q", 1, 0), ("q", 1, 1))
    project_video(1, 1)
    project_video(1, 2)
    fresh_copies = store_fresh()
    w_event(1, 0)
    x_event("kv1", 1)
    for hh in range(2):
        merge(0, hh)
    start(*[("cx", 0, dz) for dz in range(1, 4)])
    arrived(("kv1", 0), ("kv1", 5))
    for hh in range(2):
        attend(1, 0, hh, [own_block(1), groups(1, 1, 4)], True)
    arrived(("kv1", 3), ("kv1", 7))
    for hh in range(2):
        arrived(("q", 1, hh))
        attend(1, 1, hh, [groups(1, 0, 4)], True)
        attend(1, 1, hh, [groups(1, 4, 8), text_block(1)])
        give_back(1, hh)
    w_event(1, 1)
    for hh in range(2):
        attend(1, 0, hh, [groups(1, 4, 8), text_block(1)])
    load_wov.wait()
    w_event(0, 3)
    contexts_arrived(0)
    finish(0, 0)
    for hh in range(2):
        merge(1, hh)
    start(*[("cx", 1, dz) for dz in range(1, 4)])
    text_sums()
    w_event(1, 2)
    contexts_arrived(1)
    finish(1, 0)
    w_event(1, 3)
    finish(1, 1)
    finish(0, 1)
    text_pass()
    video_end(0)
    text_end()
    video_end(1)
    for copy in fresh_copies:
        copy.wait()
    for make in table.values():
        make().wait_send()


def hand_over(*refs):
    for source, target in zip(refs[:3], refs[3:]):
        target[...] = source[...]


def shards(*arrays):
    vmem = pl.BlockSpec(memory_space=pltpu.VMEM)
    hbm = pl.BlockSpec(memory_space=pl.ANY)
    scratch = [
        pltpu.VMEM((3, D, 256), BF16),
        pltpu.VMEM((3, D, 256), BF16),
        pltpu.VMEM((4, 256, D), BF16),
        pltpu.VMEM((256, D), BF16),
        pltpu.VMEM((2, VID, D), BF16),
        pltpu.VMEM((16, PIECE), F32),
        pltpu.VMEM((8, 16, PIECE), BF16),
        pltpu.VMEM((32, D), BF16),
        pltpu.VMEM((2, 2, QROWS, HD), BF16),
        pltpu.VMEM((2, 2, QROWS, HD), BF16),
        pltpu.VMEM((2, 8, 2, 2, VID, HD), BF16),
        pltpu.VMEM((2, 2, VID, HD), BF16),
        pltpu.VMEM((8, 2, 2, 2 * TXT, HD), BF16),
        pltpu.VMEM((2, 2, QROWS, HD), F32),
        pltpu.VMEM((2, 2, QROWS, HD), F32),
        pltpu.VMEM((2, 2, QROWS, HD), F32),
        pltpu.VMEM((384, 128), F32),
        pltpu.VMEM((128, 384), F32),
        pltpu.VMEM((2, 2, QROWS, HD), BF16),
        pltpu.VMEM((2, 2, QROWS, HD), BF16),
        pltpu.VMEM((2, 2, 8, 384), F32),
        pltpu.VMEM((2, 2, 8, 384), F32),
        pltpu.VMEM((2, VID, 256), BF16),
        pltpu.VMEM((2 * TXT, 256), BF16),
        pltpu.VMEM((2, 4, 2 * ROWS, 256), BF16),
        pltpu.VMEM((2, ROWS, D), F32),
        pltpu.VMEM((2, ROWS, D), BF16),
        pltpu.VMEM((2, ROWS, D), BF16),
        pltpu.VMEM((8, 16, PIECE), BF16),
        pltpu.VMEM((4, 2, 16, PIECE), BF16),
        pltpu.VMEM((16, PIECE), BF16),
        pltpu.VMEM((16, PIECE), BF16),
        pltpu.SemaphoreType.DMA((103,)),
        pltpu.SemaphoreType.DMA((103,)),
        pltpu.SemaphoreType.DMA((6,)),
        pltpu.SemaphoreType.DMA((16,)),
    ]
    out_shape = (
        jax.ShapeDtypeStruct((2, ROWS, D), BF16),
        jax.ShapeDtypeStruct((2, 2, D), BF16),
        jax.ShapeDtypeStruct((2, VID, 256), BF16),
    )
    arrays = list(arrays)
    arrays[2] = jnp.transpose(arrays[2], (1, 0, 2))
    arrays[3] = jnp.transpose(arrays[3], (1, 0, 2))
    finished = pl.pallas_call(
        kernel,
        out_shape=out_shape,
        in_specs=[vmem, vmem, vmem, vmem, hbm, hbm, hbm, hbm, vmem, hbm],
        out_specs=(vmem, vmem, hbm),
        scratch_shapes=scratch,
        compiler_params=pltpu.CompilerParams(
            collective_id=0, has_side_effects=True, vmem_limit_bytes=56 * 1024 * 1024
        ),
        cost_estimate=pl.CostEstimate(
            flops=6_000_000_000, bytes_accessed=16_000_000, transcendentals=4_800_000
        ),
    )(*arrays)
    return pl.pallas_call(
        hand_over,
        out_shape=out_shape,
        in_specs=[vmem] * 3,
        out_specs=(vmem,) * 3,
    )(*finished)


def solution(mesh):
    return jax.shard_map(
        shards,
        mesh=mesh,
        in_specs=(
            P(None, ("patch", "head"), None),
            P(None, ("patch", "head"), None),
            P(),
            P(),
            P(None, None, "head"),
            P(None, None, "head"),
            P("head", None),
            P("head", None),
            P(),
            P(None, "patch", "head"),
        ),
        out_specs=(
            P(None, ("patch", "head"), None),
            P(None, ("patch", "head"), None),
            P(None, "patch", "head"),
        ),
        check_vma=False,
    )
```

```python
import functools

import jax
import jax.numpy as jnp
from jax import lax
from jax.experimental import pallas as pl
from jax.experimental.pallas import tpu as pltpu
from jax.sharding import PartitionSpec as P

HD = 128
EPSILON = 1e-06
MESH = pl.DeviceIdType.MESH
F32 = jnp.float32
BF16 = jnp.bfloat16
EXP2_SCALE = HD ** (-0.5) * 1.4426950408889634

D = 3072
HALF = D // 2
ROWS = 32
VID = 256
TXT = 16
QROWS = VID + TXT
PIECE = 768

NEAR = 1024
FIRST, SECOND = pl.ds(0, HALF), pl.ds(HALF, HALF)


def modulated(rows, shift, scale):
    rows = rows.astype(F32)
    center = rows - jnp.mean(rows, axis=-1, keepdims=True)
    normed = center * lax.rsqrt(jnp.mean(center * center, axis=-1, keepdims=True) + EPSILON)
    return normed * (1.0 + scale) + shift


def head_norm(values, gain_row):
    return (
        values * lax.rsqrt(jnp.mean(values * values, axis=-1, keepdims=True) + EPSILON) * gain_row
    )


def piece_select(piece, transposed):
    shape = (128, 32) if transposed else (32, 128)
    row = lax.broadcasted_iota(jnp.int32, shape, 1 if transposed else 0)
    packed = lax.broadcasted_iota(jnp.int32, shape, 0 if transposed else 1)
    target = ((row & 15) >> 1) * 16 + 4 * piece + 2 * (row >> 4) + (row & 1)
    return jnp.where(packed == target, 1.0, 0.0).astype(BF16)


def slot_of(dz, fy):
    return (dz % 4) * 2 + fy


def group_of(dx, fc):
    return (dx % 4) * 2 + fc


def kernel(
    video_in,
    text_in,
    video_mod,
    text_mod,
    video_qkv,
    text_qkv,
    video_out_w,
    text_out_w,
    norm_gains,
    stale_kv,
    video_out,
    text_out,
    fresh_kv,
    wv,
    wt,
    wg,
    wot,
    xg,
    tpack,
    tg,
    tx,
    q_ref,
    q_peer,
    kvb,
    fresh,
    tkv,
    m_ref,
    l_ref,
    acc_ref,
    stat,
    stat_t,
    part_out,
    part_in,
    stat_out,
    stat_in,
    ctx,
    ctxt,
    cx,
    mine,
    give,
    last_in,
    tp,
    trx,
    text_give,
    text_last,
    send_sem,
    recv_sem,
    local_sem,
    out_sem,
):
    p = lax.axis_index("patch")
    h = lax.axis_index("head")
    x, yl, c = p // 4, (p // 2) % 2, p % 2
    yh, z = h // 4, h % 4

    def at(dx=0, fy=0, fc=0, fh=0, dz=0):
        xx = (x + dx) % 4 if dx else x
        yy = 1 - yl if fy else yl
        cc = 1 - c if fc else c
        hh = 1 - yh if fh else yh
        zz = (z + dz) % 4 if dz else z
        return (xx * 4 + yy * 2 + cc, hh * 4 + zz)

    table = {}

    def message(name, src, dst, device):
        index = len(table)

        def make():
            return pltpu.make_async_remote_copy(
                src_ref=src,
                dst_ref=dst,
                send_sem=send_sem.at[index],
                recv_sem=recv_sem.at[index],
                device_id=device,
                device_id_type=MESH,
            )

        table[name] = make

    def start(*names):
        for name in names:
            table[name]().start()

    def arrived(*names):
        for name in names:
            table[name]().wait_recv()

    zp, zm, yp = at(dz=1), at(dz=3), at(fh=1)
    xp, xm, ylp, sib = at(dx=1), at(dx=3), at(fy=1), at(fc=1)

    for s in range(2):
        def rows(dz, fy, low=0, high=D, s=s):
            return xg.at[s, pl.ds(slot_of(dz, fy) * ROWS, ROWS), pl.ds(low, high - low)]

        message(("ag", s, 0), rows(0, 0), rows(0, 1), yp)
        message(("ag", s, 1), rows(0, 0), rows(3, 0), zp)
        message(("ag", s, 2), rows(0, 0), rows(1, 0), zm)
        message(("ag", s, 3), rows(0, 1, 0, NEAR), rows(3, 1, 0, NEAR), zp)
        message(("ag", s, 4), rows(0, 1, 0, NEAR), rows(1, 1, 0, NEAR), zm)
        message(("ag", s, 5), rows(3, 0, 0, HALF), rows(2, 0, 0, HALF), zp)
        message(("ag", s, 6), rows(1, 0, HALF, D), rows(2, 0, HALF, D), zm)
        message(("ag", s, 7), rows(3, 1, 0, NEAR // 2), rows(2, 1, 0, NEAR // 2), zp)
        message(("ag", s, 8), rows(1, 1, NEAR // 2, NEAR), rows(2, 1, NEAR // 2, NEAR), zm)
        message(("ag", s, 9), rows(3, 0, NEAR, D), rows(3, 1, NEAR, D), yp)
        message(("ag", s, 10), rows(1, 0, NEAR, D), rows(1, 1, NEAR, D), yp)
        message(("ag", s, 11), rows(2, 0, NEAR, D), rows(2, 1, NEAR, D), yp)

    def gather_x(kind, block):
        message((kind, 0), block(0, 0), block(0, 1), sib)
        message((kind, 1), block(0, 0), block(3, 0), xp)
        message((kind, 2), block(0, 0), block(1, 0), xm)
        message((kind, 3), block(3, 0), block(3, 1), sib)
        message((kind, 4), block(3, 0).at[0], block(2, 0).at[0], xp)
        message((kind, 5), block(1, 0), block(1, 1), sib)
        message((kind, 6), block(1, 0).at[1], block(2, 0).at[1], xm)
        message((kind, 7), block(2, 0), block(2, 1), sib)

    gather_x("kv0", lambda dx, fc: kvb.at[0, group_of(dx, fc)])
    gather_x("kv1", lambda dx, fc: kvb.at[1, group_of(dx, fc)])
    gather_x("tkv", lambda dx, fc: tkv.at[group_of(dx, fc)])

    def x_event(kind, number):
        waits, sends = [((1, 2), (4, 6, 3, 5)), ((4, 6), (7,))][number]
        arrived(*[(kind, i) for i in waits])
        start(*[(kind, i) for i in sends])

    for s in range(2):
        for hh in range(2):
            message(("q", s, hh), q_ref.at[s, hh], q_peer.at[s, hh], ylp)
            message(("pc", s, hh), part_out.at[s, hh], part_in.at[s, hh], ylp)
            message(("st", s, hh), stat_out.at[s, hh], stat_in.at[s, hh], ylp)

    message(("ta", 0), tg.at[0], tg.at[slot_of(0, 1)], yp)
    for dz in range(1, 4):
        message(("ta", dz), tg.at[0], tg.at[slot_of(-dz, 0)], at(dz=dz))
        message(("tb", dz), tg.at[slot_of(0, 1)], tg.at[slot_of(-dz, 1)], at(dz=dz))
        message(("tr", dz), tp.at[pl.ds(slot_of(dz, 0), 2)], trx.at[(-dz) % 4], at(dz=dz))
    message(("ty",), text_give, text_last, yp)

    def piece_rows(dx, fc):
        core = 1 - c if fc else c
        return pl.ds(pl.multiple_of((((x + dx) % 4) * 2 + core) * ROWS, ROWS), ROWS)

    def weights(dx, fc, cols=pl.ds(0, D)):
        return wg.at[pl.ds(1, 3), piece_rows(dx, fc), cols]

    for part, low in enumerate((0, HALF)):
        whole, left, right = (low, HALF), (low, HALF // 2), (low + HALF // 2, HALF // 2)
        for dz in range(1, 4):
            message(
                ("wz", part, dz),
                video_out_w.at[piece_rows(0, 0), pl.ds(*whole)],
                wg.at[(-dz) % 4, piece_rows(0, 0), pl.ds(*whole)],
                at(dz=dz),
            )
        for i, (where, cols, device) in enumerate(
            [
                (0, whole, sib),
                (0, whole, xp),
                (0, whole, xm),
                (3, whole, sib),
                (3, left, xp),
                (1, whole, sib),
                (1, right, xm),
                (2, whole, sib),
            ]
        ):
            block = weights(where, 0, pl.ds(*cols))
            message(("wx", part, i), block, block, device)

    for s in range(2):
        for dz in range(1, 4):
            message(
                ("cx", s, dz),
                ctx.at[s, pl.ds(dz * 2 * ROWS, 2 * ROWS), :],
                cx.at[s, (-dz) % 4],
                at(dz=dz),
            )
        for i, cols in enumerate((FIRST, SECOND)):
            message(("yo", s, i), give.at[s, :, cols], last_in.at[s, :, cols], yp)

    barrier = pltpu.get_barrier_semaphore()
    peers = [sib, ylp, xp, xm, zp, zm, yp, at(dz=2)]
    for device in peers:
        pl.semaphore_signal(barrier, inc=1, device_id=device, device_id_type=MESH)

    loads = []

    def load(src, dst):
        copy = pltpu.make_async_copy(src, dst, local_sem.at[len(loads)])
        copy.start()
        loads.append(copy)
        return copy

    load_stale = [
        load(stale_kv.at[:, :, pl.ds(hh * HD, HD)], kvb.at[0, 0, :, hh]) for hh in range(2)
    ]
    load_wt = load(text_qkv, wt)
    load_wv = load(video_qkv, wv)
    load_wov = load(video_out_w, wg.at[0])
    load_wot = load(text_out_w, wot)

    def normalize_video(s):
        xg[s, 0:ROWS, :] = modulated(
            video_in[s], video_mod[0, s : s + 1, :], video_mod[1, s : s + 1, :]
        ).astype(BF16)

    normalize_video(0)
    for s in range(2):
        normed = modulated(text_in[s], text_mod[0, s : s + 1, :], text_mod[1, s : s + 1, :])
        for piece in range(4):
            tpack[4 * piece + 2 * s : 4 * piece + 2 * s + 2, :] = normed[
                :, piece * PIECE : (piece + 1) * PIECE
            ]
    tg[0] = tpack[...].astype(BF16)

    pl.semaphore_wait(barrier, len(peers))

    start(("ag", 0, 0), ("ag", 0, 1), ("ag", 0, 2))
    start(*[("ta", i) for i in range(4)])
    for copy in load_stale:
        copy.wait()
    start(("kv0", 1), ("kv0", 2), ("kv0", 0))
    normalize_video(1)

    def ag_event(s, number):
        waits, sends = [
            ((0,), (3, 4)),
            ((1, 2), (5, 6, 9, 10)),
            ((3, 4), (7, 8)),
            ((5, 6), (11,)),
            ((7, 8, 9, 10, 11), ()),
        ][number]
        arrived(*[("ag", s, i) for i in waits])
        start(*[("ag", s, i) for i in sends])

    def w_event(part, number):
        if number == 0:
            arrived(*[("wz", part, dz) for dz in range(1, 4)])
            start(("wx", part, 1), ("wx", part, 2), ("wx", part, 0))
        elif number == 1:
            arrived(("wx", part, 1), ("wx", part, 2))
            start(("wx", part, 4), ("wx", part, 6), ("wx", part, 3), ("wx", part, 5))
        elif number == 2:
            arrived(("wx", part, 4), ("wx", part, 6))
            start(("wx", part, 7))
        else:
            arrived(*[("wx", part, i) for i in (0, 3, 5, 7)])

    def project_text():
        arrived(*[("ta", dz) for dz in range(1, 4)], *[("tb", dz) for dz in range(1, 4)])
        packed = tg[...].reshape(128, PIECE)
        for piece in range(4):
            tx[:, piece * PIECE : (piece + 1) * PIECE] = jnp.dot(
                piece_select(piece, False), packed, preferred_element_type=F32
            ).astype(BF16)
        load_wt.wait()
        for j in range(3):
            projected = jnp.dot(tx[...], wt[j], preferred_element_type=F32)
            for hh in range(2):
                one = projected[:, hh * HD : (hh + 1) * HD]
                if j < 2:
                    one = head_norm(one, norm_gains[2 + j : 3 + j, :])
                one = one.astype(BF16)
                if j == 0:
                    for s in range(2):
                        q_ref[s, hh, VID:QROWS, :] = one[s * TXT : (s + 1) * TXT]
                else:
                    tkv[0, j - 1, hh] = one

    def project_video(s, j):
        projected = jnp.dot(xg[s], wv[j], preferred_element_type=F32)
        for hh in range(2):
            one = projected[:, hh * HD : (hh + 1) * HD]
            if j < 2:
                one = head_norm(one, norm_gains[j : j + 1, :])
            one = one.astype(BF16)
            if j == 0:
                q_ref[s, hh, 0:VID, :] = one
            elif s == 0:
                kvb[1, 0, j - 1, hh] = one
            else:
                fresh[j - 1, hh] = one

    def own_block(s):
        return lambda which, hh: kvb[1, 0, which, hh] if s == 0 else fresh[which, hh]

    def text_block(s):
        return lambda which, hh: tkv[:, which, hh, s * TXT : (s + 1) * TXT, :].reshape(8 * TXT, HD)

    def groups(s, low, high):
        return lambda which, hh: kvb[s, low:high, which, hh].reshape((high - low) * VID, HD)

    def attend(s, who, hh, blocks, is_first=False):
        keys = jnp.concatenate([block(0, hh) for block in blocks], axis=0)
        values = jnp.concatenate([block(1, hh) for block in blocks], axis=0)
        queries = q_peer[s, hh] if who else q_ref[s, hh]
        scores = lax.dot_general(
            queries, keys, (((1,), (1,)), ((), ())), preferred_element_type=F32
        )
        highest = jnp.max(scores, axis=1, keepdims=True)
        if not is_first:
            before = m_ref[who, hh][:, 0:1]
            highest = jnp.maximum(highest, before)
        weights = jnp.exp2((scores - highest) * EXP2_SCALE)
        total = jnp.sum(weights, axis=1, keepdims=True)
        mixed = jnp.dot(weights.astype(BF16), values, preferred_element_type=F32)
        if not is_first:
            shrink = jnp.exp2((before - highest) * EXP2_SCALE)
            total = total + l_ref[who, hh][:, 0:1] * shrink
            mixed = mixed + acc_ref[who, hh] * shrink
        m_ref[who, hh] = jnp.broadcast_to(highest, (QROWS, HD))
        l_ref[who, hh] = jnp.broadcast_to(total, (QROWS, HD))
        acc_ref[who, hh] = mixed

    def give_back(s, hh):
        part_out[s, hh] = (acc_ref[1, hh] / l_ref[1, hh][:, 0:1]).astype(BF16)
        lane = lax.broadcasted_iota(jnp.int32, (QROWS, HD), 1)
        stat[0:QROWS, :] = jnp.where(lane == 0, m_ref[1, hh], l_ref[1, hh])
        stat_out[s, hh] = jnp.transpose(stat[...])[0:8, :]
        start(("pc", s, hh), ("st", s, hh))

    def merge(s, hh):
        arrived(("pc", s, hh), ("st", s, hh))
        stat_t[0:8, :] = stat_in[s, hh]
        theirs = jnp.transpose(stat_t[...])[0:QROWS, :]
        m_there, l_there = theirs[:, 0:1], theirs[:, 1:2]
        m_here, l_here = m_ref[0, hh][:, 0:1], l_ref[0, hh][:, 0:1]
        highest = jnp.maximum(m_here, m_there)
        here = jnp.exp2((m_here - highest) * EXP2_SCALE)
        there = jnp.exp2((m_there - highest) * EXP2_SCALE) * l_there
        context = (acc_ref[0, hh] * here + part_in[s, hh].astype(F32) * there) / (
            l_here * here + there
        )
        context = context.astype(BF16)
        ctx[s, :, hh * HD : (hh + 1) * HD] = context[0:VID]
        ctxt[s * TXT : (s + 1) * TXT, hh * HD : (hh + 1) * HD] = context[VID:QROWS]

    def finish(s, part):
        for tile in range(3 * part, 3 * part + 3):
            cols = slice(tile * 512, (tile + 1) * 512)
            total = jnp.dot(ctx[s, 0 : 2 * ROWS, :], wg[0, :, cols], preferred_element_type=F32)
            for dz in range(1, 4):
                total = total + jnp.dot(cx[s, dz], wg[dz, :, cols], preferred_element_type=F32)
            mine[s, :, cols] = total[0:ROWS]
            give[s, :, cols] = total[ROWS : 2 * ROWS].astype(BF16)
        start(("yo", s, part))

    def contexts_arrived(s):
        arrived(*[("cx", s, dz) for dz in range(1, 4)])

    def video_end(s):
        arrived(("yo", s, 0), ("yo", s, 1))
        summed = mine[s] + last_in[s].astype(F32)
        video_out[s] = (video_in[s].astype(F32) + video_mod[2, s : s + 1, :] * summed).astype(BF16)

    def text_sums():
        load_wot.wait()
        packed = jnp.zeros((128, PIECE), F32)
        for piece in range(4):
            term = jnp.dot(
                ctxt[...],
                wot[:, piece * PIECE : (piece + 1) * PIECE],
                preferred_element_type=F32,
            ).astype(BF16)
            packed = packed + jnp.dot(
                piece_select(piece, True), term, preferred_element_type=F32
            )
        tp[...] = packed.astype(BF16).reshape(8, 16, PIECE)
        start(*[("tr", dz) for dz in range(1, 4)])

    def text_pass():
        arrived(*[("tr", dz) for dz in range(1, 4)])
        summed = tp[0:2].astype(F32)
        for dz in range(1, 4):
            summed = summed + trx[dz].astype(F32)
        tpack[...] = summed[0]
        text_give[...] = summed[1].astype(BF16)
        start(("ty",))

    def text_end():
        arrived(("ty",))
        tpack[...] = tpack[...] + text_last[...].astype(F32)
        for s in range(2):
            rows = jnp.concatenate(
                [tpack[4 * i + 2 * s : 4 * i + 2 * s + 2, :] for i in range(4)], axis=1
            )
            text_out[s] = (text_in[s].astype(F32) + text_mod[2, s : s + 1, :] * rows).astype(BF16)

    def store_fresh():
        copies = []
        for dz in range(4):
            for fy in range(2):
                slot = slot_of(dz, fy)
                owner_y = 1 - yh if fy else yh
                owner = owner_y * 4 + (z + dz) % 4
                place = pl.ds(pl.multiple_of(owner * ROWS, ROWS), ROWS)
                for hh in range(2):
                    copy = pltpu.make_async_copy(
                        fresh.at[:, hh, pl.ds(slot * ROWS, ROWS), :],
                        fresh_kv.at[:, place, pl.ds(hh * HD, HD)],
                        out_sem.at[slot * 2 + hh],
                    )
                    copy.start()
                    copies.append(copy)
        return copies

    ag_event(0, 0)
    start(("ag", 1, 0))
    ag_event(0, 1)
    start(*[("wz", 0, dz) for dz in range(1, 4)])
    arrived(("ta", 0))
    start(("tb", 1), ("tb", 2), ("tb", 3))
    x_event("kv0", 0)
    ag_event(0, 2)
    ag_event(0, 3)
    w_event(0, 0)
    x_event("kv0", 1)
    start(("ag", 1, 1), ("ag", 1, 2))
    project_text()
    start(("tkv", 1), ("tkv", 2), ("tkv", 0))
    load_wv.wait()
    ag_event(0, 4)
    project_video(0, 0)
    start(("q", 0, 0), ("q", 0, 1))
    project_video(0, 1)
    project_video(0, 2)
    start(("kv1", 1), ("kv1", 2), ("kv1", 0))
    ag_event(1, 0)
    x_event("tkv", 0)
    arrived(("kv0", 0), ("kv0", 5))
    attend(0, 0, 0, [own_block(0), groups(0, 1, 4)], True)
    ag_event(1, 1)
    start(*[("wz", 1, dz) for dz in range(1, 4)])
    attend(0, 0, 1, [own_block(0), groups(0, 1, 4)], True)
    x_event("tkv", 1)
    ag_event(1, 2)
    ag_event(1, 3)
    arrived(("kv0", 3), ("kv0", 7))
    arrived(("q", 0, 0))
    attend(0, 1, 0, [groups(0, 0, 4)], True)
    w_event(0, 1)
    arrived(*[("tkv", i) for i in (0, 3, 5, 7)])
    attend(0, 1, 0, [groups(0, 4, 8), text_block(0)])
    give_back(0, 0)
    arrived(("q", 0, 1))
    attend(0, 1, 1, [groups(0, 0, 4)], True)
    x_event("kv1", 0)
    attend(0, 1, 1, [groups(0, 4, 8), text_block(0)])
    give_back(0, 1)
    for hh in range(2):
        attend(0, 0, hh, [groups(0, 4, 8), text_block(0)])
    w_event(0, 2)
    ag_event(1, 4)
    project_video(1, 0)
    start(("q", 1, 0), ("q", 1, 1))
    project_video(1, 1)
    project_video(1, 2)
    fresh_copies = store_fresh()
    w_event(1, 0)
    x_event("kv1", 1)
    for hh in range(2):
        merge(0, hh)
    start(*[("cx", 0, dz) for dz in range(1, 4)])
    arrived(("kv1", 0), ("kv1", 5))
    for hh in range(2):
        attend(1, 0, hh, [own_block(1), groups(1, 1, 4)], True)
    arrived(("kv1", 3), ("kv1", 7))
    for hh in range(2):
        arrived(("q", 1, hh))
        attend(1, 1, hh, [groups(1, 0, 4)], True)
        attend(1, 1, hh, [groups(1, 4, 8), text_block(1)])
        give_back(1, hh)
    w_event(1, 1)
    for hh in range(2):
        attend(1, 0, hh, [groups(1, 4, 8), text_block(1)])
    load_wov.wait()
    w_event(0, 3)
    contexts_arrived(0)
    finish(0, 0)
    for hh in range(2):
        merge(1, hh)
    start(*[("cx", 1, dz) for dz in range(1, 4)])
    text_sums()
    w_event(1, 2)
    contexts_arrived(1)
    finish(1, 0)
    w_event(1, 3)
    finish(1, 1)
    finish(0, 1)
    text_pass()
    video_end(0)
    text_end()
    video_end(1)
    for copy in fresh_copies:
        copy.wait()
    for make in table.values():
        make().wait_send()


def hand_over(*refs):
    for source, target in zip(refs[:3], refs[3:]):
        target[...] = source[...]


def shards(*arrays):
    vmem = pl.BlockSpec(memory_space=pltpu.VMEM)
    hbm = pl.BlockSpec(memory_space=pl.ANY)
    scratch = [
        pltpu.VMEM((3, D, 256), BF16),
        pltpu.VMEM((3, D, 256), BF16),
        pltpu.VMEM((4, 256, D), BF16),
        pltpu.VMEM((256, D), BF16),
        pltpu.VMEM((2, VID, D), BF16),
        pltpu.VMEM((16, PIECE), F32),
        pltpu.VMEM((8, 16, PIECE), BF16),
        pltpu.VMEM((32, D), BF16),
        pltpu.VMEM((2, 2, QROWS, HD), BF16),
        pltpu.VMEM((2, 2, QROWS, HD), BF16),
        pltpu.VMEM((2, 8, 2, 2, VID, HD), BF16),
        pltpu.VMEM((2, 2, VID, HD), BF16),
        pltpu.VMEM((8, 2, 2, 2 * TXT, HD), BF16),
        pltpu.VMEM((2, 2, QROWS, HD), F32),
        pltpu.VMEM((2, 2, QROWS, HD), F32),
        pltpu.VMEM((2, 2, QROWS, HD), F32),
        pltpu.VMEM((384, 128), F32),
        pltpu.VMEM((128, 384), F32),
        pltpu.VMEM((2, 2, QROWS, HD), BF16),
        pltpu.VMEM((2, 2, QROWS, HD), BF16),
        pltpu.VMEM((2, 2, 8, 384), F32),
        pltpu.VMEM((2, 2, 8, 384), F32),
        pltpu.VMEM((2, VID, 256), BF16),
        pltpu.VMEM((2 * TXT, 256), BF16),
        pltpu.VMEM((2, 4, 2 * ROWS, 256), BF16),
        pltpu.VMEM((2, ROWS, D), F32),
        pltpu.VMEM((2, ROWS, D), BF16),
        pltpu.VMEM((2, ROWS, D), BF16),
        pltpu.VMEM((8, 16, PIECE), BF16),
        pltpu.VMEM((4, 2, 16, PIECE), BF16),
        pltpu.VMEM((16, PIECE), BF16),
        pltpu.VMEM((16, PIECE), BF16),
        pltpu.SemaphoreType.DMA((103,)),
        pltpu.SemaphoreType.DMA((103,)),
        pltpu.SemaphoreType.DMA((6,)),
        pltpu.SemaphoreType.DMA((16,)),
    ]
    out_shape = (
        jax.ShapeDtypeStruct((2, ROWS, D), BF16),
        jax.ShapeDtypeStruct((2, 2, D), BF16),
        jax.ShapeDtypeStruct((2, VID, 256), BF16),
    )
    arrays = list(arrays)
    arrays[2] = jnp.transpose(arrays[2], (1, 0, 2))
    arrays[3] = jnp.transpose(arrays[3], (1, 0, 2))
    finished = pl.pallas_call(
        kernel,
        out_shape=out_shape,
        in_specs=[vmem, vmem, vmem, vmem, hbm, hbm, hbm, hbm, vmem, hbm],
        out_specs=(vmem, vmem, hbm),
        scratch_shapes=scratch,
        compiler_params=pltpu.CompilerParams(
            collective_id=0, has_side_effects=True, vmem_limit_bytes=56 * 1024 * 1024
        ),
        cost_estimate=pl.CostEstimate(
            flops=6_000_000_000, bytes_accessed=16_000_000, transcendentals=4_800_000
        ),
    )(*arrays)
    return pl.pallas_call(
        hand_over,
        out_shape=out_shape,
        in_specs=[vmem] * 3,
        out_specs=(vmem,) * 3,
    )(*finished)


def solution(mesh):
    return jax.shard_map(
        shards,
        mesh=mesh,
        in_specs=(
            P(None, ("patch", "head"), None),
            P(None, ("patch", "head"), None),
            P(),
            P(),
            P(None, None, "head"),
            P(None, None, "head"),
            P("head", None),
            P("head", None),
            P(),
            P(None, "patch", "head"),
        ),
        out_specs=(
            P(None, ("patch", "head"), None),
            P(None, ("patch", "head"), None),
            P(None, "patch", "head"),
        ),
        check_vma=False,
    )
```
